32 devices in a mesh: space: 16 (over z, y, core), mode: 2 (over x).
Axes of the slice: x: 2, y: 2, z: 4, core: 2. Of those that a mesh axis runs over, the one named last changes fastest.
Arguments:
- guess: float32 [120, 32, 8, 128], P('mode', 'space'), may hold values from -6 to 6
- source: float32 [120, 32, 8, 128], P('mode', 'space'), may hold values from -6 to 6
- mean_coef: float32 [32, 8, 128], P('space'), may hold values from 1 to 4
- fluct_coef: float32 [7, 32, 8, 128], P(None, 'space'), may hold values from -2 to 2
- triples: int32 [3, 1680], replicated, may hold values from 0 to 119, as said below
- coupling: float32 [1680], replicated, may hold values from -1.5 to 1.5
Outputs:
- solution: float32 [120, 32, 8, 128], P('mode', 'space')
- update: float32 [120, 32, 8, 128], P('mode', 'space')
The draws below stay inside these ranges and needn't reach their ends.
Inputs may be any that keep to these rules, and one draw needn't show every extreme that they name: `triples`: row 0 holds the output mode i, row 1 the coupled mode j, row 2 the term k, which is 1 to 7; every pair (i, k) stands in exactly 2 entries, in no particular order; j is any mode.
All inputs are finite; a program needn't handle non-finite values.
Results may differ from the reference program's by a relative error of at most 0.00019.
Values sent between devices are 32-bit elements; how exact they have to be, the bound alone decides.
A program may use at most 64 MiB of HBM per device.

```python
import math
import jax
import jax.numpy as jnp
from jax import lax

P_SIZE = 120
KT = 8
S = 2
CY = 8
CZ = 128
ITERS = 3
NX = 32
NNZ = 1680


def draw_triples(key, part):
    count = P_SIZE * (KT - 1) * S
    order = jax.random.permutation(jax.random.fold_in(key, 11), count)
    first = order // ((KT - 1) * S)
    term = 1 + order // S % (KT - 1)
    partner = jax.random.randint(jax.random.fold_in(key, 12), (count,), 0, P_SIZE)
    return jnp.stack([first, partner, term]).astype(jnp.int32)


def block_scale(rng, dims, cuts, least, high):
    loudness = 1.0
    for dim, blocks in cuts:
        draws = jax.random.uniform(jax.random.fold_in(jax.random.fold_in(rng, 6), dim), (blocks,), jnp.float32, least / len(cuts), high / len(cuts))
        loudness = loudness * jnp.repeat(jnp.exp(draws), dims[dim] // blocks).reshape((-1,) + (1,) * (len(dims) - 1 - dim))
    return loudness


def scatter_about(own_key, shape, spread, reach, cuts=(), kind=jnp.bfloat16):
    array = spread * jax.random.normal(own_key, shape, jnp.float32)
    if cuts:
        array = array * block_scale(own_key, shape, cuts, -0.22, 0.18)
    return jnp.clip(array, -reach, reach).astype(kind)


def setup_inputs(seed: int = 0) -> dict:
    keys = jax.random.split(jax.random.key(seed), 7)
    return {
        "guess": scatter_about(keys[0], (P_SIZE, NX, CY, CZ), 1.0, 6.0, ((0, 2), (1, 16)), jnp.float32),
        "source": scatter_about(keys[1], (P_SIZE, NX, CY, CZ), 1.0, 6.0, ((0, 2), (1, 16)), jnp.float32),
        "mean_coef": jnp.clip(jnp.exp(math.log(4.0) - 1.3862944 * jax.random.uniform(keys[2], (NX, CY, CZ), jnp.float32) ** block_scale(keys[2], (NX, CY, CZ), ((0, 16),), -0.2, 0.2)), 1.0, 4.0),
        "fluct_coef": scatter_about(keys[3], (KT - 1, NX, CY, CZ), 0.4, 2.0, ((1, 16),), jnp.float32),
        "triples": draw_triples(jax.random.fold_in(keys[6], 71), 0),
        "coupling": scatter_about(keys[5], (NNZ,), 0.3, 1.5, (), jnp.float32),
    }


def neighbours(padded):
    centre = padded[..., 1:-1, 1:-1, 1:-1]
    others = [padded[..., 2:, 1:-1, 1:-1], padded[..., :-2, 1:-1, 1:-1],
              padded[..., 1:-1, 2:, 1:-1], padded[..., 1:-1, :-2, 1:-1],
              padded[..., 1:-1, 1:-1, 2:], padded[..., 1:-1, 1:-1, :-2]]
    return centre, others


def face_terms(padded_coef):
    centre, others = neighbours(padded_coef)
    return [0.5 * (centre + other) for other in others]


def reference(guess, source, mean_coef, fluct_coef, triples, coupling):
    coefs = jnp.concatenate([mean_coef[None], fluct_coef], axis=0)
    faces = face_terms(jnp.pad(coefs, ((0, 0), (1, 1), (1, 1), (1, 1))))
    diagonal = faces[0][0]
    for face in faces[1:]:
        diagonal = diagonal + face[0]
    table = jnp.zeros((P_SIZE, KT, P_SIZE), jnp.float32).at[triples[0], triples[2], triples[1]].add(coupling)
    table = table.at[:, 0, :].add(jnp.eye(P_SIZE, dtype=jnp.float32))
    solution = guess
    update = guess
    for step in range(ITERS):
        flat = solution.reshape(P_SIZE, -1)

        def one_mode(row):
            mixed = jnp.dot(row, flat, precision=lax.Precision.HIGHEST).reshape((KT,) + solution.shape[1:])
            padded = jnp.pad(mixed, ((0, 0), (1, 1), (1, 1), (1, 1)))
            centre, others = neighbours(padded)
            total = jnp.zeros(solution.shape[1:], jnp.float32)
            for face, other in zip(faces, others):
                total = total + jnp.sum(face * (centre - other), axis=0)
            return total

        image = lax.map(one_mode, table)
        update = (source - image) / diagonal
        solution = solution + 0.5 * update
    return (solution, update)
```

```python
import functools

import jax
import jax.numpy as jnp
from jax import lax
from jax.experimental import pallas as pl
from jax.experimental.pallas import tpu as pltpu
from jax.sharding import PartitionSpec as P

ITERS = 3
MESH = pl.DeviceIdType.MESH
SUB = 8
ROWS = 32


def kernel(dims, guess, source, mean, fluct, triples, coupling, sol_out, upd_out,
           field, rhs, pack_g, pack_s, back_s, back_u, last, coef, tile, faces, inverse,
           pattern, table, fine, coarse, plain,
           coef_sem, guess_sem, rhs_sem, rim_sem, x_sem, y_sem, sol_sem, upd_sem):
    slabs, groups, blocks, room, planes, rows, depth, terms, entries = dims
    share = rows // groups
    width = room * groups
    f32, bf16 = jnp.float32, jnp.bfloat16
    here = lax.axis_index("space")
    me = lax.axis_index("mode")
    has_prev, has_next = here > 0, here < slabs - 1
    has_left, has_right = me > 0, me < groups - 1
    even = lax.rem(here, 2) == 0

    def remote(src, dst, sems, index, space, mode):
        return pltpu.make_async_remote_copy(
            src_ref=src, dst_ref=dst, send_sem=sems.at[(0,) + index], recv_sem=sems.at[(1,) + index],
            device_id={"space": space, "mode": mode}, device_id_type=MESH)

    def group(offset):
        return lax.rem(me + offset + groups, groups)

    def block(owner):
        return pl.ds(pl.multiple_of(owner * room, SUB), room)

    def plane_at(q):
        return jnp.where(even, planes - 1 - q, q)

    @pl.when(here == 0)
    def _():
        field[:, 0] = jnp.zeros((ITERS, share + 2, width, depth), f32)
        coef[:, 0] = jnp.zeros((terms, rows, depth), f32)

    @pl.when(here == slabs - 1)
    def _():
        field[:, planes + 1] = jnp.zeros((ITERS, share + 2, width, depth), f32)
        coef[:, planes + 1] = jnp.zeros((terms, rows, depth), f32)

    @pl.when(me == 0)
    def _():
        field[:, 1:planes + 1, 0] = jnp.zeros((ITERS, planes, width, depth), f32)

    @pl.when(me == groups - 1)
    def _():
        field[:, 1:planes + 1, share + 1] = jnp.zeros((ITERS, planes, width, depth), f32)

    barrier = pltpu.get_barrier_semaphore()

    @pl.when(has_prev)
    def _():
        pl.semaphore_signal(barrier, inc=1, device_id={"space": here - 1, "mode": me}, device_id_type=MESH)

    @pl.when(has_next)
    def _():
        pl.semaphore_signal(barrier, inc=1, device_id={"space": here + 1, "mode": me}, device_id_type=MESH)

    for d in range(1, groups):
        pl.semaphore_signal(barrier, inc=1, device_id={"space": here, "mode": group(d)}, device_id_type=MESH)

    tall = share + 1 if groups == 2 else share + 2

    def first_row(owner):
        return jnp.where(owner > 0, 0, 1) if groups == 2 else 0

    gap = jnp.zeros((room - blocks, depth), f32)

    def rows_of(ref, p, y):
        part = ref[pl.ds(p * rows + y, blocks, stride=planes * rows), :]
        return jnp.concatenate([part, gap], axis=0) if room > blocks else part

    for t in range(groups):
        for p in range(planes):
            for r in range(share + 2):
                y = t * share + r - 1
                if 0 <= y < rows:
                    pack_g[t, p, r] = rows_of(guess, p, y)
                elif groups != 2:
                    pack_g[t, p, r] = jnp.zeros((room, depth), f32)

    pl.semaphore_wait(barrier, groups - 1 + has_prev.astype(jnp.int32) + has_next.astype(jnp.int32))

    def coef_copies(up):
        at, to, space = (planes - 1, 0, here + 1) if up else (0, planes + 1, here - 1)
        way = 0 if up else 1
        return [
            remote(mean.at[at], coef.at[0, to], coef_sem, (way, 0), space, me),
            remote(fluct.at[:, at], coef.at[pl.ds(1, terms - 1), to], coef_sem, (way, 1), space, me),
        ]

    def guess_copy(d, p, owner, target):
        start = first_row(target)
        return remote(
            pack_g.at[target, p, pl.ds(start, tall)],
            field.at[0, p + 1, pl.ds(start, tall), block(owner)],
            guess_sem, (d, p), here, target)

    for q in range(planes):
        p = plane_at(planes - 1 - q)
        for d in range(1, groups):
            guess_copy(d, p, me, group(d)).start()

    @pl.when(has_next)
    def _():
        for copy in coef_copies(True):
            copy.start()

    @pl.when(has_prev)
    def _():
        for copy in coef_copies(False):
            copy.start()

    def rim_copy(up, d, owner):
        at, to, space = (planes, 0, here + 1) if up else (1, planes + 1, here - 1)
        span = pl.ds(1, share)
        return remote(field.at[0, at, span, block(owner)], field.at[0, to, span, block(owner)],
                      rim_sem, (0 if up else 1, d), space, me)

    for p in range(planes):
        for r in range(tall):
            at = first_row(me) + r
            field[0, p + 1, at, block(me)] = pack_g[me, p, at]

    @pl.when(has_next)
    def _():
        rim_copy(True, 0, me).start()

    @pl.when(has_prev)
    def _():
        rim_copy(False, 0, me).start()

    for t in range(groups):
        for p in range(planes):
            for r in range(share):
                pack_s[t, p, r] = rows_of(source, p, t * share + r)
    rhs[:, :, block(me)] = pack_s[me]

    pattern[...] = jnp.full(pattern.shape, -1, jnp.int32)
    pattern[0:3, 0:entries] = triples[...]
    length = pattern.shape[1]

    def spread(i):
        shift = jnp.zeros_like(i)
        for g in range(1, groups):
            shift = shift + jnp.where(i >= g * blocks, room - blocks, 0)
        return i + shift

    owner_row = spread(pattern[0:1, :])
    column = spread(pattern[1:2, :]) + (pattern[2:3, :] - 1) * width
    value = jnp.concatenate([coupling[...], jnp.zeros((1, length - entries), f32)], axis=1)
    high = value.astype(bf16).astype(f32)
    low = value - high
    hit = lax.broadcasted_iota(jnp.int32, (width, length), 0) == owner_row
    picks = jnp.concatenate(
        [jnp.where(hit, high, 0.0).astype(bf16), jnp.where(hit, low, 0.0).astype(bf16)], axis=0)

    for k in range(terms - 1):
        chosen = lax.broadcasted_iota(jnp.int32, (width, length), 0) + k * width == column
        chosen = jnp.where(chosen, 1.0, 0.0).astype(bf16)
        both = lax.dot_general(picks, chosen, (((1,), (1,)), ((), ())), preferred_element_type=f32)
        entry = both[:width] + both[width:]
        top = entry.astype(bf16)
        table[:width, k * width:(k + 1) * width] = top
        table[width:, k * width:(k + 1) * width] = (entry - top.astype(f32)).astype(bf16)

    def rhs_copy(d, owner, target):
        return remote(pack_s.at[target], rhs.at[:, :, block(owner)], rhs_sem, (d,), here, target)

    for d in range(1, groups):
        owner = group(-d)
        for p in range(planes):
            guess_copy(d, p, owner, me).wait_recv()

        @pl.when(has_next)
        def _():
            rim_copy(True, d, owner).start()

        @pl.when(has_prev)
        def _():
            rim_copy(False, d, owner).start()

    for d in range(1, groups):
        rhs_copy(d, me, group(d)).start()

    coef[0, 1:planes + 1] = mean[...]
    coef[1:, 1:planes + 1] = fluct[...]

    @pl.when(has_prev)
    def _():
        for copy in coef_copies(True):
            copy.wait_recv()

    @pl.when(has_next)
    def _():
        for copy in coef_copies(False):
            copy.wait_recv()

    def face_step(k, p):
        a = coef[k, p + 1]
        row = lax.broadcasted_iota(jnp.int32, a.shape, 0)
        lane = lax.broadcasted_iota(jnp.int32, a.shape, 1)
        tile[0] = 0.5 * (a + coef[k, p + 2])
        tile[1] = 0.5 * (a + coef[k, p])
        tile[2] = 0.5 * (a + jnp.where(row == rows - 1, 0.0, pltpu.roll(a, rows - 1, 0)))
        tile[3] = 0.5 * (a + jnp.where(row == 0, 0.0, pltpu.roll(a, 1, 0)))
        tile[4] = 0.5 * (a + jnp.where(lane == depth - 1, 0.0, pltpu.roll(a, depth - 1, 1)))
        tile[5] = 0.5 * (a + jnp.where(lane == 0, 0.0, pltpu.roll(a, 1, 1)))
        for r in range(share):
            for n in range(6):
                faces[p, r, k, n] = jnp.broadcast_to(tile[n, pl.ds(me * share + r, 1), :], (SUB, depth))

    def face_loop(k, carry):
        for p in range(planes):
            face_step(k, p)
        return carry

    lax.fori_loop(0, terms, face_loop, 0)
    for p in range(planes):
        for r in range(share):
            total = faces[p, r, 0, 0]
            for n in range(1, 6):
                total = total + faces[p, r, 0, n]
            inverse[p, r] = 1.0 / total

    lane = lax.broadcasted_iota(jnp.int32, (ROWS, depth), 1)

    def gather_terms(step, p):
        def by_block(index, carry):
            r = index // (width // ROWS)
            begin = pl.multiple_of(lax.rem(index, width // ROWS) * ROWS, ROWS)

            def cells(a, b):
                return field[step, a, b, pl.ds(begin, ROWS), :]

            centre = cells(p + 1, r + 1)
            others = [
                cells(p + 2, r + 1), cells(p, r + 1), cells(p + 1, r + 2), cells(p + 1, r),
                jnp.where(lane == depth - 1, 0.0, pltpu.roll(centre, depth - 1, 1)),
                jnp.where(lane == 0, 0.0, pltpu.roll(centre, 1, 1)),
            ]
            drops = [(centre - other).reshape(ROWS // SUB, SUB, depth) for other in others]
            for k in range(terms):
                acc = faces[p, r, k, 0][None] * drops[0]
                for n in range(1, 6):
                    acc = acc + faces[p, r, k, n][None] * drops[n]
                acc = acc.reshape(ROWS, depth)
                if k == 0:
                    plain[r, pl.ds(begin, ROWS), :] = acc
                else:
                    top = acc.astype(bf16)
                    at = pl.ds(pl.multiple_of((k - 1) * width + begin, ROWS), ROWS)
                    lanes = pl.ds(pl.multiple_of(r * depth, depth), depth)
                    coarse[at, lanes] = top
                    fine[at, lanes] = (acc - top.astype(f32)).astype(bf16)
            return carry

        lax.fori_loop(0, share * (width // ROWS), by_block, 0)

    def x_copy(step, up):
        at, to, space = (planes, 0, here + 1) if up else (1, planes + 1, here - 1)
        span = pl.ds(1, share)
        return remote(field.at[step, at, span], field.at[step, to, span],
                      x_sem, (step, 0 if up else 1), space, me)

    def y_copy(step, p, right):
        at, to, mode = (share, 0, me + 1) if right else (1, share + 1, me - 1)
        return remote(field.at[step, p + 1, at], field.at[step, p + 1, to],
                      y_sem, (step, 0 if right else 1, p), here, mode)

    def sol_copy(d, p, slot, target):
        return remote(field.at[ITERS - 1, p + 1, pl.ds(1, share), block(target)], back_s.at[slot, p],
                      sol_sem, (d, p), here, target)

    def upd_copy(d, p, slot, target):
        return remote(last.at[p, :, block(target)], back_u.at[slot, p], upd_sem, (d, p), here, target)

    def await_rims(step, p):
        @pl.when((p == 0) & has_prev)
        def _():
            if step == 0:
                for d in range(groups):
                    rim_copy(True, d, group(-d)).wait_recv()
            else:
                x_copy(step, True).wait_recv()

        @pl.when((p == planes - 1) & has_next)
        def _():
            if step == 0:
                for d in range(groups):
                    rim_copy(False, d, group(-d)).wait_recv()
            else:
                x_copy(step, False).wait_recv()

        if step > 0:
            @pl.when(has_left)
            def _():
                y_copy(step, p, True).wait_recv()

            @pl.when(has_right)
            def _():
                y_copy(step, p, False).wait_recv()

    for step in range(ITERS):
        def sweep(q, carry, step=step):
            p = plane_at(q)
            await_rims(step, p)
            gather_terms(step, p)
            both = jnp.dot(table[...], coarse[...], preferred_element_type=f32)
            image = both[:width] + both[width:]
            image = image + jnp.dot(table[:width], fine[...], preferred_element_type=f32)
            if step == 0:
                @pl.when(q == 0)
                def _():
                    for d in range(1, groups):
                        rhs_copy(d, group(-d), me).wait_recv()
            for r in range(share):
                rest = rhs[p, r] - plain[r] - image[:, r * depth:(r + 1) * depth]
                rest = rest.reshape(width // SUB, SUB, depth) * inverse[p, r][None]
                rest = rest.reshape(width, depth)
                if step < ITERS - 1:
                    field[step + 1, p + 1, r + 1] = field[step, p + 1, r + 1] + 0.5 * rest
                else:
                    last[p, r] = rest
            if step < ITERS - 1:
                @pl.when((p == planes - 1) & has_next)
                def _():
                    x_copy(step + 1, True).start()

                @pl.when((p == 0) & has_prev)
                def _():
                    x_copy(step + 1, False).start()

                @pl.when(has_right)
                def _():
                    y_copy(step + 1, p, True).start()

                @pl.when(has_left)
                def _():
                    y_copy(step + 1, p, False).start()

            if step == ITERS - 2:
                for d in range(1, groups):
                    sol_copy(d, p, me, group(d)).start()
            if step == ITERS - 1:
                for d in range(1, groups):
                    upd_copy(d, p, me, group(d)).start()
            return carry

        lax.fori_loop(0, planes, sweep, 0)

    for p in range(planes):
        back_s[me, p] = field[ITERS - 1, p + 1, 1:share + 1, block(me)]
        back_u[me, p] = last[p, :, block(me)]
    for d in range(1, groups):
        for p in range(planes):
            sol_copy(d, p, group(-d), me).wait_recv()
            upd_copy(d, p, group(-d), me).wait_recv()
    for g in range(groups):
        for p in range(planes):
            for r in range(share):
                at = pl.ds(p * rows + g * share + r, blocks, stride=planes * rows)
                change = back_u[g, p, r][:blocks]
                upd_out[at, :] = change
                sol_out[at, :] = back_s[g, p, r][:blocks] + 0.5 * change

    for d in range(1, groups):
        for p in range(planes):
            guess_copy(d, p, me, group(d)).wait_send()
            sol_copy(d, p, me, group(d)).wait_send()
            upd_copy(d, p, me, group(d)).wait_send()
        rhs_copy(d, me, group(d)).wait_send()
    for up, has in ((True, has_next), (False, has_prev)):
        @pl.when(has)
        def _():
            for copy in coef_copies(up):
                copy.wait_send()
            for d in range(groups):
                rim_copy(up, d, group(-d)).wait_send()
            for step in range(1, ITERS):
                x_copy(step, up).wait_send()
    for right, has in ((True, has_right), (False, has_left)):
        @pl.when(has)
        def _():
            for step in range(1, ITERS):
                for p in range(planes):
                    y_copy(step, p, right).wait_send()


def per_device(guess, source, mean_coef, fluct_coef, triples, coupling):
    blocks, planes, rows, depth = guess.shape
    groups, slabs = lax.axis_size("mode"), lax.axis_size("space")
    terms = fluct_coef.shape[0] + 1
    entries = triples.shape[1]
    share = rows // groups
    room = -(-blocks // 16) * 16
    while (room * groups) % 128:
        room += 16
    width = room * groups
    length = -(-entries // 128) * 128
    f32, bf16 = jnp.float32, jnp.bfloat16
    dims = (slabs, groups, blocks, room, planes, rows, depth, terms, entries)
    flat = jax.ShapeDtypeStruct((blocks * planes * rows, depth), f32)
    dma = pltpu.SemaphoreType.DMA
    vmem = pl.BlockSpec(memory_space=pltpu.VMEM)
    solution, update = pl.pallas_call(
        functools.partial(kernel, dims),
        out_shape=(flat, flat),
        in_specs=[vmem] * 6,
        out_specs=(vmem, vmem),
        scratch_shapes=[
            pltpu.VMEM((ITERS, planes + 2, share + 2, width, depth), f32),
            pltpu.VMEM((planes, share, width, depth), f32),
            pltpu.VMEM((groups, planes, share + 2, room, depth), f32),
            pltpu.VMEM((groups, planes, share, room, depth), f32),
            pltpu.VMEM((groups, planes, share, room, depth), f32),
            pltpu.VMEM((groups, planes, share, room, depth), f32),
            pltpu.VMEM((planes, share, width, depth), f32),
            pltpu.VMEM((terms, planes + 2, rows, depth), f32),
            pltpu.VMEM((6, rows, depth), f32),
            pltpu.VMEM((planes, share, terms, 6, SUB, depth), f32),
            pltpu.VMEM((planes, share, SUB, depth), f32),
            pltpu.VMEM((SUB, length), jnp.int32),
            pltpu.VMEM((2 * width, (terms - 1) * width), bf16),
            pltpu.VMEM(((terms - 1) * width, share * depth), bf16),
            pltpu.VMEM(((terms - 1) * width, share * depth), bf16),
            pltpu.VMEM((share, width, depth), f32),
            dma((2, 2, 2)),
            dma((2, groups, planes)),
            dma((2, groups)),
            dma((2, 2, groups)),
            dma((2, ITERS, 2)),
            dma((2, ITERS, 2, planes)),
            dma((2, groups, planes)),
            dma((2, groups, planes)),
        ],
        compiler_params=pltpu.CompilerParams(
            collective_id=0, has_side_effects=True, vmem_limit_bytes=48 * 1024 * 1024
        ),
    )(
        guess.reshape(flat.shape),
        source.reshape(flat.shape),
        mean_coef,
        fluct_coef,
        triples,
        coupling.reshape(1, entries),
    )
    return solution.reshape(guess.shape), update.reshape(guess.shape)


def solution(mesh):
    in_specs = (
        P("mode", "space", None, None),
        P("mode", "space", None, None),
        P("space", None, None),
        P(None, "space", None, None),
        P(),
        P(),
    )
    out_specs = (P("mode", "space", None, None), P("mode", "space", None, None))
    return jax.shard_map(
        per_device, mesh=mesh, in_specs=in_specs, out_specs=out_specs, check_vma=False
    )
```

```python
import functools

import jax
import jax.numpy as jnp
from jax import lax
from jax.experimental import pallas as pl
from jax.experimental.pallas import tpu as pltpu
from jax.sharding import PartitionSpec as P

ITERS = 3
MESH = pl.DeviceIdType.MESH
SUB = 8
ROWS = 32


def kernel(dims, guess_in, source_in, mean_in, fluct_in, triples_in, coupling_in, sol_out, upd_out,
           guess, source, triples, coupling, in_sem,
           field, rhs, pack_g, pack_s, back_s, back_u, last, coef, tile, faces, inverse,
           pattern, table, fine, coarse, plain,
           coef_sem, guess_sem, rhs_sem, rim_sem, x_sem, y_sem, sol_sem, upd_sem):
    slabs, groups, blocks, room, planes, rows, depth, terms, entries = dims
    share = rows // groups
    band = 2 if share % 2 == 0 else 1
    bands = share // band
    width = room * groups
    f32, bf16 = jnp.float32, jnp.bfloat16
    here = lax.axis_index("space")
    me = lax.axis_index("mode")
    has_prev, has_next = here > 0, here < slabs - 1
    has_left, has_right = me > 0, me < groups - 1
    even = lax.rem(here, 2) == 0

    def remote(src, dst, sems, index, space, mode):
        return pltpu.make_async_remote_copy(
            src_ref=src, dst_ref=dst, send_sem=sems.at[(0,) + index], recv_sem=sems.at[(1,) + index],
            device_id={"space": space, "mode": mode}, device_id_type=MESH)

    def group(offset):
        return lax.rem(me + offset + groups, groups)

    def block(owner):
        return pl.ds(pl.multiple_of(owner * room, SUB), room)

    def plane_at(q):
        return jnp.where(even, planes - 1 - q, q)

    inputs = [
        pltpu.make_async_copy(guess_in, guess, in_sem.at[0]),
        pltpu.make_async_copy(mean_in, coef.at[0, pl.ds(1, planes)], in_sem.at[1]),
        pltpu.make_async_copy(fluct_in, coef.at[pl.ds(1, terms - 1), pl.ds(1, planes)], in_sem.at[2]),
        pltpu.make_async_copy(source_in, source, in_sem.at[3]),
        pltpu.make_async_copy(triples_in, triples, in_sem.at[4]),
        pltpu.make_async_copy(coupling_in, coupling, in_sem.at[5]),
    ]
    for copy in inputs:
        copy.start()

    @pl.when(here == 0)
    def _():
        field[:, 0] = jnp.zeros((ITERS, share + 2, width, depth), f32)
        coef[:, 0] = jnp.zeros((terms, rows, depth), f32)

    @pl.when(here == slabs - 1)
    def _():
        field[:, planes + 1] = jnp.zeros((ITERS, share + 2, width, depth), f32)
        coef[:, planes + 1] = jnp.zeros((terms, rows, depth), f32)

    @pl.when(me == 0)
    def _():
        field[:, 1:planes + 1, 0] = jnp.zeros((ITERS, planes, width, depth), f32)

    @pl.when(me == groups - 1)
    def _():
        field[:, 1:planes + 1, share + 1] = jnp.zeros((ITERS, planes, width, depth), f32)

    barrier = pltpu.get_barrier_semaphore()

    @pl.when(has_prev)
    def _():
        pl.semaphore_signal(barrier, inc=1, device_id={"space": here - 1, "mode": me}, device_id_type=MESH)

    @pl.when(has_next)
    def _():
        pl.semaphore_signal(barrier, inc=1, device_id={"space": here + 1, "mode": me}, device_id_type=MESH)

    for d in range(1, groups):
        pl.semaphore_signal(barrier, inc=1, device_id={"space": here, "mode": group(d)}, device_id_type=MESH)

    tall = share + 1 if groups == 2 else share + 2

    def first_row(owner):
        return jnp.where(owner > 0, 0, 1) if groups == 2 else 0

    gap = jnp.zeros((room - blocks, depth), f32)

    def rows_of(ref, p, y):
        part = ref[pl.ds(p * rows + y, blocks, stride=planes * rows), :]
        return jnp.concatenate([part, gap], axis=0) if room > blocks else part

    def coef_copy(up):
        at, to, space = (planes, 0, here + 1) if up else (1, planes + 1, here - 1)
        return remote(coef.at[:, at], coef.at[:, to], coef_sem, (0 if up else 1,), space, me)

    def guess_copy(d, p, owner, target):
        start = first_row(target)
        return remote(
            pack_g.at[target, p, pl.ds(start, tall)],
            field.at[0, p + 1, pl.ds(start, tall), block(owner)],
            guess_sem, (d, p), here, target)

    def guess_row(p, target, at):
        y = target * share + at - 1
        inside = jnp.clip(y, 0, rows - 1)
        part = rows_of(guess, p, inside)
        return part if groups == 2 else jnp.where(y == inside, part, 0.0)

    inputs[0].wait()
    for q in range(planes):
        p = plane_at(planes - 1 - q)
        for d in range(1, groups):
            target = group(d)
            for r in range(tall):
                at = first_row(target) + r
                pack_g[target, p, at] = guess_row(p, target, at)
            if q == 0 and d == 1:
                pl.semaphore_wait(
                    barrier, groups - 1 + has_prev.astype(jnp.int32) + has_next.astype(jnp.int32))
            guess_copy(d, p, me, target).start()

    inputs[1].wait()
    inputs[2].wait()

    @pl.when(has_next)
    def _():
        coef_copy(True).start()

    @pl.when(has_prev)
    def _():
        coef_copy(False).start()

    def rim_copy(up, d, owner):
        at, to, space = (planes, 0, here + 1) if up else (1, planes + 1, here - 1)
        span = pl.ds(1, share)
        return remote(field.at[0, at, span, block(owner)], field.at[0, to, span, block(owner)],
                      rim_sem, (0 if up else 1, d), space, me)

    for p in range(planes):
        for r in range(tall):
            at = first_row(me) + r
            field[0, p + 1, at, block(me)] = guess_row(p, me, at)

    @pl.when(has_next)
    def _():
        rim_copy(True, 0, me).start()

    @pl.when(has_prev)
    def _():
        rim_copy(False, 0, me).start()

    inputs[3].wait()
    for d in range(groups):
        target = group(d)
        for p in range(planes):
            for r in range(share):
                part = rows_of(source, p, target * share + r)
                if d == 0:
                    rhs[p, r, block(me)] = part
                else:
                    pack_s[target, p, r] = part

    inputs[4].wait()
    inputs[5].wait()
    pattern[...] = jnp.full(pattern.shape, -1, jnp.int32)
    pattern[0:3, 0:entries] = triples[...]
    length = pattern.shape[1]

    def spread(i):
        shift = jnp.zeros_like(i)
        for g in range(1, groups):
            shift = shift + jnp.where(i >= g * blocks, room - blocks, 0)
        return i + shift

    owner_row = spread(pattern[0:1, :])
    column = spread(pattern[1:2, :]) + (pattern[2:3, :] - 1) * width
    value = jnp.concatenate([coupling[...].reshape(1, entries), jnp.zeros((1, length - entries), f32)], axis=1)
    high = value.astype(bf16).astype(f32)
    low = value - high
    hit = lax.broadcasted_iota(jnp.int32, (width, length), 0) == owner_row
    picks = jnp.concatenate(
        [jnp.where(hit, high, 0.0).astype(bf16), jnp.where(hit, low, 0.0).astype(bf16)], axis=0)

    for k in range(terms - 1):
        chosen = lax.broadcasted_iota(jnp.int32, (width, length), 0) + k * width == column
        chosen = jnp.where(chosen, 1.0, 0.0).astype(bf16)
        both = lax.dot_general(picks, chosen, (((1,), (1,)), ((), ())), preferred_element_type=f32)
        entry = both[:width] + both[width:]
        top = entry.astype(bf16)
        table[:width, k * width:(k + 1) * width] = top
        table[width:, k * width:(k + 1) * width] = (entry - top.astype(f32)).astype(bf16)

    def rhs_copy(d, owner, target):
        return remote(pack_s.at[target], rhs.at[:, :, block(owner)], rhs_sem, (d,), here, target)

    for q in range(planes):
        p = plane_at(planes - 1 - q)
        for d in range(1, groups):
            owner = group(-d)
            guess_copy(d, p, owner, me).wait_recv()

            @pl.when((p == planes - 1) & has_next)
            def _():
                rim_copy(True, d, owner).start()

            @pl.when((p == 0) & has_prev)
            def _():
                rim_copy(False, d, owner).start()

    for d in range(1, groups):
        rhs_copy(d, me, group(d)).start()

    @pl.when(has_prev)
    def _():
        coef_copy(True).wait_recv()

    @pl.when(has_next)
    def _():
        coef_copy(False).wait_recv()

    def face_step(k, p):
        a = coef[k, p + 1]
        row = lax.broadcasted_iota(jnp.int32, a.shape, 0)
        lane = lax.broadcasted_iota(jnp.int32, a.shape, 1)
        tile[0] = 0.5 * (a + coef[k, p + 2])
        tile[1] = 0.5 * (a + coef[k, p])
        tile[2] = 0.5 * (a + jnp.where(row == rows - 1, 0.0, pltpu.roll(a, rows - 1, 0)))
        tile[3] = 0.5 * (a + jnp.where(row == 0, 0.0, pltpu.roll(a, 1, 0)))
        tile[4] = 0.5 * (a + jnp.where(lane == depth - 1, 0.0, pltpu.roll(a, depth - 1, 1)))
        tile[5] = 0.5 * (a + jnp.where(lane == 0, 0.0, pltpu.roll(a, 1, 1)))
        for r in range(share):
            for n in range(6):
                faces[p, r, k, n] = jnp.broadcast_to(tile[n, pl.ds(me * share + r, 1), :], (SUB, depth))

    def face_loop(k, carry):
        for p in range(planes):
            face_step(k, p)
        return carry

    lax.fori_loop(0, terms, face_loop, 0)
    for p in range(planes):
        for r in range(share):
            total = faces[p, r, 0, 0]
            for n in range(1, 6):
                total = total + faces[p, r, 0, n]
            inverse[p, r] = 1.0 / total

    lane = lax.broadcasted_iota(jnp.int32, (ROWS, depth), 1)

    def gather_terms(step, p, base):
        def by_block(index, carry):
            line = index // (width // ROWS)
            r = base + line
            begin = pl.multiple_of(lax.rem(index, width // ROWS) * ROWS, ROWS)

            def cells(a, b):
                return field[step, a, b, pl.ds(begin, ROWS), :]

            centre = cells(p + 1, r + 1)
            others = [
                cells(p + 2, r + 1), cells(p, r + 1), cells(p + 1, r + 2), cells(p + 1, r),
                jnp.where(lane == depth - 1, 0.0, pltpu.roll(centre, depth - 1, 1)),
                jnp.where(lane == 0, 0.0, pltpu.roll(centre, 1, 1)),
            ]
            drops = [(centre - other).reshape(ROWS // SUB, SUB, depth) for other in others]
            for k in range(terms):
                acc = faces[p, r, k, 0][None] * drops[0]
                for n in range(1, 6):
                    acc = acc + faces[p, r, k, n][None] * drops[n]
                acc = acc.reshape(ROWS, depth)
                if k == 0:
                    plain[line, pl.ds(begin, ROWS), :] = acc
                else:
                    top = acc.astype(bf16)
                    at = pl.ds(pl.multiple_of((k - 1) * width + begin, ROWS), ROWS)
                    lanes = pl.ds(pl.multiple_of(line * depth, depth), depth)
                    coarse[at, lanes] = top
                    fine[at, lanes] = (acc - top.astype(f32)).astype(bf16)
            return carry

        lax.fori_loop(0, band * (width // ROWS), by_block, 0)

    def x_copy(step, up, part):
        at, to, space = (planes, 0, here + 1) if up else (1, planes + 1, here - 1)
        span = pl.ds(1 + part * band, band)
        return remote(field.at[step, at, span], field.at[step, to, span],
                      x_sem, (step, 0 if up else 1, part), space, me)

    def y_copy(step, p, right):
        at, to, mode = (share, 0, me + 1) if right else (1, share + 1, me - 1)
        return remote(field.at[step, p + 1, at], field.at[step, p + 1, to],
                      y_sem, (step, 0 if right else 1, p), here, mode)

    def sol_copy(d, p, slot, target):
        return remote(field.at[ITERS - 1, p + 1, pl.ds(1, share), block(target)], back_s.at[slot, p],
                      sol_sem, (d, p), here, target)

    def upd_copy(d, p, part, slot, target):
        span = pl.ds(part * band, band)
        return remote(last.at[p, span, block(target)], back_u.at[slot, p, span],
                      upd_sem, (d, p, part), here, target)

    def await_rims(step, p, part):
        first = part == 0

        @pl.when((p == 0) & has_prev)
        def _():
            if step == 0:
                @pl.when(first)
                def _():
                    for d in range(groups):
                        rim_copy(True, d, group(-d)).wait_recv()
            else:
                x_copy(step, True, part).wait_recv()

        @pl.when((p == planes - 1) & has_next)
        def _():
            if step == 0:
                @pl.when(first)
                def _():
                    for d in range(groups):
                        rim_copy(False, d, group(-d)).wait_recv()
            else:
                x_copy(step, False, part).wait_recv()

        if step > 0:
            @pl.when(has_left & first)
            def _():
                y_copy(step, p, True).wait_recv()

            @pl.when(has_right & (part == bands - 1))
            def _():
                y_copy(step, p, False).wait_recv()

    for step in range(ITERS):
        def sweep(unit, carry, step=step):
            q, part = unit // bands, lax.rem(unit, bands)
            p = plane_at(q)
            base = part * band
            await_rims(step, p, part)
            if step == ITERS - 1:
                @pl.when(unit == planes * bands - 1)
                def _():
                    for d in range(1, groups):
                        sol_copy(d, p, me, group(d)).start()
            gather_terms(step, p, base)
            both = jnp.dot(table[...], coarse[...], preferred_element_type=f32)
            image = both[:width] + both[width:]
            image = image + jnp.dot(table[:width], fine[...], preferred_element_type=f32)
            if step == 0:
                @pl.when(unit == 0)
                def _():
                    for d in range(1, groups):
                        rhs_copy(d, group(-d), me).wait_recv()
            for line in range(band):
                r = base + line
                rest = rhs[p, r] - plain[line] - image[:, line * depth:(line + 1) * depth]
                rest = rest.reshape(width // SUB, SUB, depth) * inverse[p, r][None]
                rest = rest.reshape(width, depth)
                if step < ITERS - 1:
                    field[step + 1, p + 1, r + 1] = field[step, p + 1, r + 1] + 0.5 * rest
                else:
                    last[p, r] = rest
            if step < ITERS - 1:
                @pl.when((p == planes - 1) & has_next)
                def _():
                    x_copy(step + 1, True, part).start()

                @pl.when((p == 0) & has_prev)
                def _():
                    x_copy(step + 1, False, part).start()

                @pl.when(has_right & (part == bands - 1))
                def _():
                    y_copy(step + 1, p, True).start()

                @pl.when(has_left & (part == 0))
                def _():
                    y_copy(step + 1, p, False).start()

            if step == ITERS - 2:
                @pl.when((part == bands - 1) & (q < planes - 1))
                def _():
                    for d in range(1, groups):
                        sol_copy(d, p, me, group(d)).start()
            if step == ITERS - 1:
                for d in range(1, groups):
                    upd_copy(d, p, part, me, group(d)).start()
            return carry

        lax.fori_loop(0, planes * bands, sweep, 0)

    def write(p, g, lines, base, change, start):
        for r in range(lines):
            at = pl.ds(p * rows + g * share + base + r, blocks, stride=planes * rows)
            upd_out[at, :] = change[r][:blocks]
            sol_out[at, :] = start[r][:blocks] + 0.5 * change[r][:blocks]

    for p in range(planes):
        write(p, me, share, 0, last[p, :, block(me)],
              field[ITERS - 1, p + 1, 1:share + 1, block(me)])
    for q in range(planes):
        p = plane_at(q)
        for d in range(1, groups):
            g = group(-d)
            sol_copy(d, p, g, me).wait_recv()
            for part in range(bands):
                upd_copy(d, p, part, g, me).wait_recv()
                span = pl.ds(part * band, band)
                write(p, g, band, part * band, back_u[g, p, span], back_s[g, p, span])

    for d in range(1, groups):
        for p in range(planes):
            guess_copy(d, p, me, group(d)).wait_send()
            sol_copy(d, p, me, group(d)).wait_send()
            for part in range(bands):
                upd_copy(d, p, part, me, group(d)).wait_send()
        rhs_copy(d, me, group(d)).wait_send()
    for up, has in ((True, has_next), (False, has_prev)):
        @pl.when(has)
        def _():
            coef_copy(up).wait_send()
            for d in range(groups):
                rim_copy(up, d, group(-d)).wait_send()
            for step in range(1, ITERS):
                for part in range(bands):
                    x_copy(step, up, part).wait_send()
    for right, has in ((True, has_right), (False, has_left)):
        @pl.when(has)
        def _():
            for step in range(1, ITERS):
                for p in range(planes):
                    y_copy(step, p, right).wait_send()


def per_device(guess, source, mean_coef, fluct_coef, triples, coupling):
    blocks, planes, rows, depth = guess.shape
    groups, slabs = lax.axis_size("mode"), lax.axis_size("space")
    terms = fluct_coef.shape[0] + 1
    entries = triples.shape[1]
    share = rows // groups
    band = 2 if share % 2 == 0 else 1
    room = -(-blocks // 16) * 16
    while (room * groups) % 128:
        room += 16
    width = room * groups
    length = -(-entries // 128) * 128
    f32, bf16 = jnp.float32, jnp.bfloat16
    dims = (slabs, groups, blocks, room, planes, rows, depth, terms, entries)
    flat = jax.ShapeDtypeStruct((blocks * planes * rows, depth), f32)
    dma = pltpu.SemaphoreType.DMA
    vmem = pl.BlockSpec(memory_space=pltpu.VMEM)
    solution, update = pl.pallas_call(
        functools.partial(kernel, dims),
        out_shape=(flat, flat),
        in_specs=[pl.BlockSpec(memory_space=pltpu.HBM)] * 6,
        out_specs=(vmem, vmem),
        scratch_shapes=[
            pltpu.VMEM(flat.shape, f32),
            pltpu.VMEM(flat.shape, f32),
            pltpu.VMEM(triples.shape, jnp.int32),
            pltpu.VMEM(coupling.shape, f32),
            dma((6,)),
            pltpu.VMEM((ITERS, planes + 2, share + 2, width, depth), f32),
            pltpu.VMEM((planes, share, width, depth), f32),
            pltpu.VMEM((groups, planes, share + 2, room, depth), f32),
            pltpu.VMEM((groups, planes, share, room, depth), f32),
            pltpu.VMEM((groups, planes, share, room, depth), f32),
            pltpu.VMEM((groups, planes, share, room, depth), f32),
            pltpu.VMEM((planes, share, width, depth), f32),
            pltpu.VMEM((terms, planes + 2, rows, depth), f32),
            pltpu.VMEM((6, rows, depth), f32),
            pltpu.VMEM((planes, share, terms, 6, SUB, depth), f32),
            pltpu.VMEM((planes, share, SUB, depth), f32),
            pltpu.VMEM((SUB, length), jnp.int32),
            pltpu.VMEM((2 * width, (terms - 1) * width), bf16),
            pltpu.VMEM(((terms - 1) * width, band * depth), bf16),
            pltpu.VMEM(((terms - 1) * width, band * depth), bf16),
            pltpu.VMEM((band, width, depth), f32),
            dma((2, 2)),
            dma((2, groups, planes)),
            dma((2, groups)),
            dma((2, 2, groups)),
            dma((2, ITERS, 2, share // band)),
            dma((2, ITERS, 2, planes)),
            dma((2, groups, planes)),
            dma((2, groups, planes, share // band)),
        ],
        compiler_params=pltpu.CompilerParams(
            collective_id=0, has_side_effects=True, vmem_limit_bytes=62 * 1024 * 1024
        ),
    )(
        guess.reshape(flat.shape),
        source.reshape(flat.shape),
        mean_coef,
        fluct_coef,
        triples,
        coupling,
    )
    return solution.reshape(guess.shape), update.reshape(guess.shape)


def solution(mesh):
    in_specs = (
        P("mode", "space", None, None),
        P("mode", "space", None, None),
        P("space", None, None),
        P(None, "space", None, None),
        P(),
        P(),
    )
    out_specs = (P("mode", "space", None, None), P("mode", "space", None, None))
    return jax.shard_map(
        per_device, mesh=mesh, in_specs=in_specs, out_specs=out_specs, check_vma=False
    )
```

```python
import functools

import jax
import jax.numpy as jnp
from jax import lax
from jax.experimental import pallas as pl
from jax.experimental.pallas import tpu as pltpu
from jax.sharding import PartitionSpec as P

ITERS = 3
MESH = pl.DeviceIdType.MESH
SUB = 8
ROWS = 32


def kernel(dims, guess_in, source_in, mean_in, fluct_in, triples_in, coupling_in, sol_out, rest_out, diagonal,
           guess, source, triples, coupling, in_sem,
           field, rhs, pack_g, pack_s, back_s, back_u, last, coef, tile, faces, inverse,
           pattern, table, plain,
           coef_sem, guess_sem, rhs_sem, rim_sem, x_sem, y_sem, sol_sem, upd_sem):
    slabs, groups, blocks, room, planes, rows, depth, terms, entries = dims
    share = rows // groups
    band = 2 if share % 2 == 0 else 1
    bands = share // band
    width = room * groups
    f32, bf16 = jnp.float32, jnp.bfloat16
    here = lax.axis_index("space")
    me = lax.axis_index("mode")
    has_prev, has_next = here > 0, here < slabs - 1
    has_left, has_right = me > 0, me < groups - 1
    even = lax.rem(here, 2) == 0

    def remote(src, dst, sems, index, space, mode):
        return pltpu.make_async_remote_copy(
            src_ref=src, dst_ref=dst, send_sem=sems.at[(0,) + index], recv_sem=sems.at[(1,) + index],
            device_id={"space": space, "mode": mode}, device_id_type=MESH)

    def group(offset):
        return lax.rem(me + offset + groups, groups)

    def block(owner):
        return pl.ds(pl.multiple_of(owner * room, SUB), room)

    def plane_at(q):
        return jnp.where(even, planes - 1 - q, q)

    inputs = [
        pltpu.make_async_copy(guess_in, guess, in_sem.at[0]),
        pltpu.make_async_copy(mean_in, coef.at[0, pl.ds(1, planes)], in_sem.at[1]),
        pltpu.make_async_copy(fluct_in, coef.at[pl.ds(1, terms - 1), pl.ds(1, planes)], in_sem.at[2]),
        pltpu.make_async_copy(source_in, source, in_sem.at[3]),
        pltpu.make_async_copy(triples_in, triples, in_sem.at[4]),
        pltpu.make_async_copy(coupling_in, coupling, in_sem.at[5]),
    ]
    for copy in inputs:
        copy.start()

    @pl.when(here == 0)
    def _():
        field[:, 0] = jnp.zeros((ITERS, share + 2, width, depth), f32)
        coef[:, 0] = jnp.zeros((terms, rows, depth), f32)

    @pl.when(here == slabs - 1)
    def _():
        field[:, planes + 1] = jnp.zeros((ITERS, share + 2, width, depth), f32)
        coef[:, planes + 1] = jnp.zeros((terms, rows, depth), f32)

    @pl.when(me == 0)
    def _():
        field[:, 1:planes + 1, 0] = jnp.zeros((ITERS, planes, width, depth), f32)

    @pl.when(me == groups - 1)
    def _():
        field[:, 1:planes + 1, share + 1] = jnp.zeros((ITERS, planes, width, depth), f32)

    barrier = pltpu.get_barrier_semaphore()

    @pl.when(has_prev)
    def _():
        pl.semaphore_signal(barrier, inc=1, device_id={"space": here - 1, "mode": me}, device_id_type=MESH)

    @pl.when(has_next)
    def _():
        pl.semaphore_signal(barrier, inc=1, device_id={"space": here + 1, "mode": me}, device_id_type=MESH)

    for d in range(1, groups):
        pl.semaphore_signal(barrier, inc=1, device_id={"space": here, "mode": group(d)}, device_id_type=MESH)

    tall = share + 1 if groups == 2 else share + 2

    def first_row(owner):
        return jnp.where(owner > 0, 0, 1) if groups == 2 else 0

    gap = jnp.zeros((room - blocks, depth), f32)

    def rows_of(ref, p, y):
        part = ref[pl.ds(p * rows + y, blocks, stride=planes * rows), :]
        return jnp.concatenate([part, gap], axis=0) if room > blocks else part

    def coef_copy(up):
        at, to, space = (planes, 0, here + 1) if up else (1, planes + 1, here - 1)
        return remote(coef.at[:, at], coef.at[:, to], coef_sem, (0 if up else 1,), space, me)

    def guess_copy(d, p, owner, target):
        start = first_row(target)
        return remote(
            pack_g.at[target, p, pl.ds(start, tall)],
            field.at[0, p + 1, pl.ds(start, tall), block(owner)],
            guess_sem, (d, p), here, target)

    def guess_row(p, target, at):
        y = target * share + at - 1
        inside = jnp.clip(y, 0, rows - 1)
        part = rows_of(guess, p, inside)
        return part if groups == 2 else jnp.where(y == inside, part, 0.0)

    inputs[0].wait()
    for q in range(planes):
        p = plane_at(planes - 1 - q)
        for d in range(1, groups):
            target = group(d)
            for r in range(tall):
                at = first_row(target) + r
                pack_g[target, p, at] = guess_row(p, target, at)
            if q == 0 and d == 1:
                pl.semaphore_wait(
                    barrier, groups - 1 + has_prev.astype(jnp.int32) + has_next.astype(jnp.int32))
            guess_copy(d, p, me, target).start()

    inputs[1].wait()
    inputs[2].wait()

    @pl.when(has_next)
    def _():
        coef_copy(True).start()

    @pl.when(has_prev)
    def _():
        coef_copy(False).start()

    def rim_copy(up, d, owner):
        at, to, space = (planes, 0, here + 1) if up else (1, planes + 1, here - 1)
        span = pl.ds(1, share)
        return remote(field.at[0, at, span, block(owner)], field.at[0, to, span, block(owner)],
                      rim_sem, (0 if up else 1, d), space, me)

    for p in range(planes):
        for r in range(tall):
            at = first_row(me) + r
            field[0, p + 1, at, block(me)] = guess_row(p, me, at)

    @pl.when(has_next)
    def _():
        rim_copy(True, 0, me).start()

    @pl.when(has_prev)
    def _():
        rim_copy(False, 0, me).start()

    inputs[3].wait()
    for d in range(groups):
        target = group(d)
        for p in range(planes):
            for r in range(share):
                part = rows_of(source, p, target * share + r)
                if d == 0:
                    rhs[p, r, block(me)] = part
                else:
                    pack_s[target, p, r] = part

    inputs[4].wait()
    inputs[5].wait()
    pattern[...] = jnp.full(pattern.shape, -1, jnp.int32)
    pattern[0:3, 0:entries] = triples[...]
    length = pattern.shape[1]

    def spread(i):
        shift = jnp.zeros_like(i)
        for g in range(1, groups):
            shift = shift + jnp.where(i >= g * blocks, room - blocks, 0)
        return i + shift

    owner_row = spread(pattern[0:1, :])
    partner = spread(pattern[1:2, :])
    chunk = (terms - 1) * ROWS
    column = partner + (partner // ROWS) * (chunk - ROWS) + (pattern[2:3, :] - 1) * ROWS
    value = jnp.concatenate([coupling[...].reshape(1, entries), jnp.zeros((1, length - entries), f32)], axis=1)
    high = value.astype(bf16).astype(f32)
    low = value - high
    hit = lax.broadcasted_iota(jnp.int32, (width, length), 0) == owner_row
    picks = jnp.concatenate(
        [jnp.where(hit, high, 0.0).astype(bf16), jnp.where(hit, low, 0.0).astype(bf16)], axis=0)
    order = lax.broadcasted_iota(jnp.int32, (chunk, length), 0)
    for b in range(width // ROWS):
        chosen = jnp.where(order == column - b * chunk, 1.0, 0.0).astype(bf16)
        both = lax.dot_general(picks, chosen, (((1,), (1,)), ((), ())), preferred_element_type=f32)
        entry = both[:width] + both[width:]
        top = entry.astype(bf16)
        table[b, :width, :] = top
        table[b, width:, :] = (entry - top.astype(f32)).astype(bf16)

    @pl.when(has_prev)
    def _():
        coef_copy(True).wait_recv()

    @pl.when(has_next)
    def _():
        coef_copy(False).wait_recv()

    def face_step(k, p):
        a = coef[k, p + 1]
        row = lax.broadcasted_iota(jnp.int32, a.shape, 0)
        lane = lax.broadcasted_iota(jnp.int32, a.shape, 1)
        tile[0] = 0.5 * (a + coef[k, p + 2])
        tile[1] = 0.5 * (a + coef[k, p])
        tile[2] = 0.5 * (a + jnp.where(row == rows - 1, 0.0, pltpu.roll(a, rows - 1, 0)))
        tile[3] = 0.5 * (a + jnp.where(row == 0, 0.0, pltpu.roll(a, 1, 0)))
        tile[4] = 0.5 * (a + jnp.where(lane == depth - 1, 0.0, pltpu.roll(a, depth - 1, 1)))
        tile[5] = 0.5 * (a + jnp.where(lane == 0, 0.0, pltpu.roll(a, 1, 1)))

        @pl.when(k == 0)
        def _():
            total = tile[0]
            for n in range(1, 6):
                total = total + tile[n]
            diagonal[p] = total

        for r in range(share):
            for n in range(6):
                faces[p, r, k, n] = jnp.broadcast_to(tile[n, pl.ds(me * share + r, 1), :], (SUB, depth))

    def face_loop(k, carry):
        for p in range(planes):
            face_step(k, p)
        return carry

    lax.fori_loop(0, terms, face_loop, 0)
    for p in range(planes):
        for r in range(share):
            total = faces[p, r, 0, 0]
            for n in range(1, 6):
                total = total + faces[p, r, 0, n]
            inverse[p, r] = 1.0 / total

    def rhs_copy(d, owner, target):
        return remote(pack_s.at[target], rhs.at[:, :, block(owner)], rhs_sem, (d,), here, target)

    for q in range(planes):
        p = plane_at(planes - 1 - q)
        for d in range(1, groups):
            owner = group(-d)
            guess_copy(d, p, owner, me).wait_recv()

            @pl.when((p == planes - 1) & has_next)
            def _():
                rim_copy(True, d, owner).start()

            @pl.when((p == 0) & has_prev)
            def _():
                rim_copy(False, d, owner).start()

    for d in range(1, groups):
        rhs_copy(d, me, group(d)).start()

    lane = lax.broadcasted_iota(jnp.int32, (ROWS, depth), 1)

    def mix(step, p, base):
        image = jnp.zeros((width, band * depth), f32)
        second = jnp.zeros((width, band * depth), f32)
        for b in range(width // ROWS):
            begin = b * ROWS
            tops, rests = [], []
            for line in range(band):
                r = base + line

                def cells(x, y):
                    return field[step, x, y, begin:begin + ROWS, :]

                centre = cells(p + 1, r + 1)
                others = [
                    cells(p + 2, r + 1), cells(p, r + 1), cells(p + 1, r + 2), cells(p + 1, r),
                    jnp.where(lane == depth - 1, 0.0, pltpu.roll(centre, depth - 1, 1)),
                    jnp.where(lane == 0, 0.0, pltpu.roll(centre, 1, 1)),
                ]
                drops = [(centre - other).reshape(ROWS // SUB, SUB, depth) for other in others]
                highs, lows = [], []
                for k in range(terms):
                    acc = faces[p, r, k, 0][None] * drops[0]
                    for n in range(1, 6):
                        acc = acc + faces[p, r, k, n][None] * drops[n]
                    acc = acc.reshape(ROWS, depth)
                    if k == 0:
                        plain[line, begin:begin + ROWS, :] = acc
                    else:
                        top = acc.astype(bf16)
                        highs.append(top)
                        lows.append((acc - top.astype(f32)).astype(bf16))
                tops.append(jnp.concatenate(highs, axis=0))
                rests.append(jnp.concatenate(lows, axis=0))
            coarse = jnp.concatenate(tops, axis=1)
            fine = jnp.concatenate(rests, axis=1)
            both = jnp.dot(table[b], coarse, preferred_element_type=f32)
            image = image + both[:width] + jnp.dot(table[b, :width], fine, preferred_element_type=f32)
            second = second + both[width:]
        return image + second

    def x_copy(step, up, part):
        at, to, space = (planes, 0, here + 1) if up else (1, planes + 1, here - 1)
        span = pl.ds(1 + part * band, band)
        return remote(field.at[step, at, span], field.at[step, to, span],
                      x_sem, (step, 0 if up else 1, part), space, me)

    def y_copy(step, p, right):
        at, to, mode = (share, 0, me + 1) if right else (1, share + 1, me - 1)
        return remote(field.at[step, p + 1, at], field.at[step, p + 1, to],
                      y_sem, (step, 0 if right else 1, p), here, mode)

    def sol_copy(d, p, slot, target):
        return remote(field.at[ITERS - 1, p + 1, pl.ds(1, share), block(target)], back_s.at[slot, p],
                      sol_sem, (d, p), here, target)

    def upd_copy(d, p, part, slot, target):
        span = pl.ds(part * band, band)
        return remote(last.at[p, span, block(target)], back_u.at[slot, p, span],
                      upd_sem, (d, p, part), here, target)

    def await_rims(step, p, part):
        first = part == 0

        @pl.when((p == 0) & has_prev)
        def _():
            if step == 0:
                @pl.when(first)
                def _():
                    for d in range(groups):
                        rim_copy(True, d, group(-d)).wait_recv()
            else:
                x_copy(step, True, part).wait_recv()

        @pl.when((p == planes - 1) & has_next)
        def _():
            if step == 0:
                @pl.when(first)
                def _():
                    for d in range(groups):
                        rim_copy(False, d, group(-d)).wait_recv()
            else:
                x_copy(step, False, part).wait_recv()

        if step > 0:
            @pl.when(has_left & first)
            def _():
                y_copy(step, p, True).wait_recv()

            @pl.when(has_right & (part == bands - 1))
            def _():
                y_copy(step, p, False).wait_recv()

    for step in range(ITERS):
        def sweep(unit, carry, step=step):
            q, part = unit // bands, lax.rem(unit, bands)
            p = plane_at(q)
            base = part * band
            await_rims(step, p, part)
            if step == ITERS - 1:
                @pl.when(unit == planes * bands - 1)
                def _():
                    for d in range(1, groups):
                        sol_copy(d, p, me, group(d)).start()
            image = mix(step, p, base)
            if step == 0:
                @pl.when(unit == 0)
                def _():
                    for d in range(1, groups):
                        rhs_copy(d, group(-d), me).wait_recv()
            for line in range(band):
                r = base + line
                rest = rhs[p, r] - plain[line] - image[:, line * depth:(line + 1) * depth]
                if step < ITERS - 1:
                    rest = rest.reshape(width // SUB, SUB, depth) * inverse[p, r][None]
                    rest = rest.reshape(width, depth)
                    field[step + 1, p + 1, r + 1] = field[step, p + 1, r + 1] + 0.5 * rest
                else:
                    last[p, r] = rest
            if step < ITERS - 1:
                @pl.when((p == planes - 1) & has_next)
                def _():
                    x_copy(step + 1, True, part).start()

                @pl.when((p == 0) & has_prev)
                def _():
                    x_copy(step + 1, False, part).start()

                @pl.when(has_right & (part == bands - 1))
                def _():
                    y_copy(step + 1, p, True).start()

                @pl.when(has_left & (part == 0))
                def _():
                    y_copy(step + 1, p, False).start()

            if step == ITERS - 2:
                @pl.when((part == bands - 1) & (q < planes - 1))
                def _():
                    for d in range(1, groups):
                        sol_copy(d, p, me, group(d)).start()
            if step == ITERS - 1:
                for d in range(1, groups):
                    upd_copy(d, p, part, me, group(d)).start()
            return carry

        lax.fori_loop(0, planes * bands, sweep, 0)

    def write(out, p, g, lines, base, cells):
        for r in range(lines):
            at = pl.ds(p * rows + g * share + base + r, blocks, stride=planes * rows)
            out[at, :] = cells[r][:blocks]

    for p in range(planes):
        write(rest_out, p, me, share, 0, last[p, :, block(me)])
        write(sol_out, p, me, share, 0, field[ITERS - 1, p + 1, 1:share + 1, block(me)])
    for q in range(planes):
        p = plane_at(q)
        for d in range(1, groups):
            g = group(-d)
            sol_copy(d, p, g, me).wait_recv()
            write(sol_out, p, g, share, 0, back_s[g, p])
    for q in range(planes):
        p = plane_at(q)
        for d in range(1, groups):
            g = group(-d)
            for part in range(bands):
                upd_copy(d, p, part, g, me).wait_recv()
                write(rest_out, p, g, band, part * band, back_u[g, p, pl.ds(part * band, band)])

    for d in range(1, groups):
        for p in range(planes):
            guess_copy(d, p, me, group(d)).wait_send()
            sol_copy(d, p, me, group(d)).wait_send()
            for part in range(bands):
                upd_copy(d, p, part, me, group(d)).wait_send()
        rhs_copy(d, me, group(d)).wait_send()
    for up, has in ((True, has_next), (False, has_prev)):
        @pl.when(has)
        def _():
            coef_copy(up).wait_send()
            for d in range(groups):
                rim_copy(up, d, group(-d)).wait_send()
            for step in range(1, ITERS):
                for part in range(bands):
                    x_copy(step, up, part).wait_send()
    for right, has in ((True, has_right), (False, has_left)):
        @pl.when(has)
        def _():
            for step in range(1, ITERS):
                for p in range(planes):
                    y_copy(step, p, right).wait_send()


def per_device(guess, source, mean_coef, fluct_coef, triples, coupling):
    blocks, planes, rows, depth = guess.shape
    groups, slabs = lax.axis_size("mode"), lax.axis_size("space")
    terms = fluct_coef.shape[0] + 1
    entries = triples.shape[1]
    share = rows // groups
    band = 2 if share % 2 == 0 else 1
    room = -(-blocks // 16) * 16
    while (room * groups) % 128:
        room += 16
    width = room * groups
    length = -(-entries // 128) * 128
    f32, bf16 = jnp.float32, jnp.bfloat16
    dims = (slabs, groups, blocks, room, planes, rows, depth, terms, entries)
    flat = jax.ShapeDtypeStruct((blocks * planes * rows, depth), f32)
    dma = pltpu.SemaphoreType.DMA
    vmem = pl.BlockSpec(memory_space=pltpu.VMEM)
    base, rest, diagonal = pl.pallas_call(
        functools.partial(kernel, dims),
        out_shape=(flat, flat, jax.ShapeDtypeStruct((planes, rows, depth), f32)),
        in_specs=[pl.BlockSpec(memory_space=pltpu.HBM)] * 6,
        out_specs=(vmem, vmem, vmem),
        scratch_shapes=[
            pltpu.VMEM(flat.shape, f32),
            pltpu.VMEM(flat.shape, f32),
            pltpu.VMEM(triples.shape, jnp.int32),
            pltpu.VMEM(coupling.shape, f32),
            dma((6,)),
            pltpu.VMEM((ITERS, planes + 2, share + 2, width, depth), f32),
            pltpu.VMEM((planes, share, width, depth), f32),
            pltpu.VMEM((groups, planes, share + 2, room, depth), f32),
            pltpu.VMEM((groups, planes, share, room, depth), f32),
            pltpu.VMEM((groups, planes, share, room, depth), f32),
            pltpu.VMEM((groups, planes, share, room, depth), f32),
            pltpu.VMEM((planes, share, width, depth), f32),
            pltpu.VMEM((terms, planes + 2, rows, depth), f32),
            pltpu.VMEM((6, rows, depth), f32),
            pltpu.VMEM((planes, share, terms, 6, SUB, depth), f32),
            pltpu.VMEM((planes, share, SUB, depth), f32),
            pltpu.VMEM((SUB, length), jnp.int32),
            pltpu.VMEM((width // ROWS, 2 * width, (terms - 1) * ROWS), bf16),
            pltpu.VMEM((band, width, depth), f32),
            dma((2, 2)),
            dma((2, groups, planes)),
            dma((2, groups)),
            dma((2, 2, groups)),
            dma((2, ITERS, 2, share // band)),
            dma((2, ITERS, 2, planes)),
            dma((2, groups, planes)),
            dma((2, groups, planes, share // band)),
        ],
        compiler_params=pltpu.CompilerParams(
            collective_id=0, has_side_effects=True, vmem_limit_bytes=62 * 1024 * 1024
        ),
    )(
        guess.reshape(flat.shape),
        source.reshape(flat.shape),
        mean_coef,
        fluct_coef,
        triples,
        coupling,
    )
    update = rest.reshape(guess.shape) / diagonal
    return base.reshape(guess.shape) + 0.5 * update, update


def solution(mesh):
    in_specs = (
        P("mode", "space", None, None),
        P("mode", "space", None, None),
        P("space", None, None),
        P(None, "space", None, None),
        P(),
        P(),
    )
    out_specs = (P("mode", "space", None, None), P("mode", "space", None, None))
    return jax.shard_map(
        per_device, mesh=mesh, in_specs=in_specs, out_specs=out_specs, check_vma=False
    )
```

```python
import functools

import jax
import jax.numpy as jnp
from jax import lax
from jax.experimental import pallas as pl
from jax.experimental.pallas import tpu as pltpu
from jax.sharding import PartitionSpec as P

ITERS = 3
MESH = pl.DeviceIdType.MESH
SUB = 8
ROWS = 32


def kernel(dims, guess_in, source_in, mean_in, fluct_in, triples_in, coupling_in, sol_out, half_out,
           guess, source, triples, coupling, in_sem,
           field, rhs, pack_g, pack_s, back_s, back_u, last, coef, tile, faces, inverse,
           pattern, table, plain,
           coef_sem, guess_sem, rhs_sem, rim_sem, x_sem, y_sem, sol_sem, upd_sem):
    slabs, groups, blocks, room, planes, rows, depth, terms, entries = dims
    share = rows // groups
    band = 2 if share % 2 == 0 else 1
    bands = share // band
    width = room * groups
    f32, bf16 = jnp.float32, jnp.bfloat16
    here = lax.axis_index("space")
    me = lax.axis_index("mode")
    has_prev, has_next = here > 0, here < slabs - 1
    has_left, has_right = me > 0, me < groups - 1
    even = lax.rem(here, 2) == 0

    def remote(src, dst, sems, index, space, mode):
        return pltpu.make_async_remote_copy(
            src_ref=src, dst_ref=dst, send_sem=sems.at[(0,) + index], recv_sem=sems.at[(1,) + index],
            device_id={"space": space, "mode": mode}, device_id_type=MESH)

    def group(offset):
        return lax.rem(me + offset + groups, groups)

    def block(owner):
        return pl.ds(pl.multiple_of(owner * room, SUB), room)

    def plane_at(q):
        return jnp.where(even, planes - 1 - q, q)

    inputs = [
        pltpu.make_async_copy(guess_in, guess, in_sem.at[0]),
        pltpu.make_async_copy(mean_in, coef.at[0, pl.ds(1, planes)], in_sem.at[1]),
        pltpu.make_async_copy(fluct_in, coef.at[pl.ds(1, terms - 1), pl.ds(1, planes)], in_sem.at[2]),
        pltpu.make_async_copy(source_in, source, in_sem.at[3]),
        pltpu.make_async_copy(triples_in, triples, in_sem.at[4]),
        pltpu.make_async_copy(coupling_in, coupling, in_sem.at[5]),
    ]
    for copy in inputs:
        copy.start()

    @pl.when(here == 0)
    def _():
        field[:, 0] = jnp.zeros((ITERS, share + 2, width, depth), f32)
        coef[:, 0] = jnp.zeros((terms, rows, depth), f32)

    @pl.when(here == slabs - 1)
    def _():
        field[:, planes + 1] = jnp.zeros((ITERS, share + 2, width, depth), f32)
        coef[:, planes + 1] = jnp.zeros((terms, rows, depth), f32)

    @pl.when(me == 0)
    def _():
        field[:, 1:planes + 1, 0] = jnp.zeros((ITERS, planes, width, depth), f32)

    @pl.when(me == groups - 1)
    def _():
        field[:, 1:planes + 1, share + 1] = jnp.zeros((ITERS, planes, width, depth), f32)

    barrier = pltpu.get_barrier_semaphore()

    @pl.when(has_prev)
    def _():
        pl.semaphore_signal(barrier, inc=1, device_id={"space": here - 1, "mode": me}, device_id_type=MESH)

    @pl.when(has_next)
    def _():
        pl.semaphore_signal(barrier, inc=1, device_id={"space": here + 1, "mode": me}, device_id_type=MESH)

    for d in range(1, groups):
        pl.semaphore_signal(barrier, inc=1, device_id={"space": here, "mode": group(d)}, device_id_type=MESH)

    tall = share + 1 if groups == 2 else share + 2

    def first_row(owner):
        return jnp.where(owner > 0, 0, 1) if groups == 2 else 0

    gap = jnp.zeros((room - blocks, depth), f32)

    def rows_of(ref, p, y):
        part = ref[pl.ds(p * rows + y, blocks, stride=planes * rows), :]
        return jnp.concatenate([part, gap], axis=0) if room > blocks else part

    def coef_copy(up):
        at, to, space = (planes, 0, here + 1) if up else (1, planes + 1, here - 1)
        return remote(coef.at[:, at], coef.at[:, to], coef_sem, (0 if up else 1,), space, me)

    def guess_copy(d, p, owner, target):
        start = first_row(target)
        return remote(
            pack_g.at[target, p, pl.ds(start, tall)],
            field.at[0, p + 1, pl.ds(start, tall), block(owner)],
            guess_sem, (d, p), here, target)

    def guess_row(p, target, at):
        y = target * share + at - 1
        inside = jnp.clip(y, 0, rows - 1)
        part = rows_of(guess, p, inside)
        return part if groups == 2 else jnp.where(y == inside, part, 0.0)

    inputs[0].wait()
    for q in range(planes):
        p = plane_at(planes - 1 - q)
        for d in range(1, groups):
            target = group(d)
            for r in range(tall):
                at = first_row(target) + r
                pack_g[target, p, at] = guess_row(p, target, at)
            if q == 0 and d == 1:
                pl.semaphore_wait(
                    barrier, groups - 1 + has_prev.astype(jnp.int32) + has_next.astype(jnp.int32))
            guess_copy(d, p, me, target).start()

    inputs[1].wait()
    inputs[2].wait()

    @pl.when(has_next)
    def _():
        coef_copy(True).start()

    @pl.when(has_prev)
    def _():
        coef_copy(False).start()

    def rim_copy(up, d, owner):
        at, to, space = (planes, 0, here + 1) if up else (1, planes + 1, here - 1)
        span = pl.ds(1, share)
        return remote(field.at[0, at, span, block(owner)], field.at[0, to, span, block(owner)],
                      rim_sem, (0 if up else 1, d), space, me)

    for p in range(planes):
        for r in range(tall):
            at = first_row(me) + r
            field[0, p + 1, at, block(me)] = guess_row(p, me, at)

    @pl.when(has_next)
    def _():
        rim_copy(True, 0, me).start()

    @pl.when(has_prev)
    def _():
        rim_copy(False, 0, me).start()

    inputs[3].wait()
    for d in range(groups):
        target = group(d)
        for p in range(planes):
            for r in range(share):
                part = rows_of(source, p, target * share + r)
                if d == 0:
                    rhs[p, r, block(me)] = part
                else:
                    pack_s[target, p, r] = part

    inputs[4].wait()
    inputs[5].wait()
    pattern[...] = jnp.full(pattern.shape, -1, jnp.int32)
    pattern[0:3, 0:entries] = triples[...]
    length = pattern.shape[1]

    def spread(i):
        shift = jnp.zeros_like(i)
        for g in range(1, groups):
            shift = shift + jnp.where(i >= g * blocks, room - blocks, 0)
        return i + shift

    owner_row = spread(pattern[0:1, :])
    partner = spread(pattern[1:2, :])
    chunk = (terms - 1) * ROWS
    column = partner + (partner // ROWS) * (chunk - ROWS) + (pattern[2:3, :] - 1) * ROWS
    value = jnp.concatenate([coupling[...].reshape(1, entries), jnp.zeros((1, length - entries), f32)], axis=1)
    high = value.astype(bf16).astype(f32)
    low = value - high
    hit = lax.broadcasted_iota(jnp.int32, (width, length), 0) == owner_row
    picks = jnp.concatenate(
        [jnp.where(hit, high, 0.0).astype(bf16), jnp.where(hit, low, 0.0).astype(bf16)], axis=0)
    order = lax.broadcasted_iota(jnp.int32, (chunk, length), 0)
    for b in range(width // ROWS):
        chosen = jnp.where(order == column - b * chunk, 1.0, 0.0).astype(bf16)
        both = lax.dot_general(picks, chosen, (((1,), (1,)), ((), ())), preferred_element_type=f32)
        entry = both[:width] + both[width:]
        top = entry.astype(bf16)
        table[b, :width, :] = top
        table[b, width:, :] = (entry - top.astype(f32)).astype(bf16)

    def rhs_copy(d, owner, target):
        return remote(pack_s.at[target], rhs.at[:, :, block(owner)], rhs_sem, (d,), here, target)

    for d in range(1, groups):
        rhs_copy(d, me, group(d)).start()

    @pl.when(has_prev)
    def _():
        coef_copy(True).wait_recv()

    @pl.when(has_next)
    def _():
        coef_copy(False).wait_recv()

    def face_step(k, p):
        a = coef[k, p + 1]
        row = lax.broadcasted_iota(jnp.int32, a.shape, 0)
        lane = lax.broadcasted_iota(jnp.int32, a.shape, 1)
        tile[0] = 0.5 * (a + coef[k, p + 2])
        tile[1] = 0.5 * (a + coef[k, p])
        tile[2] = 0.5 * (a + jnp.where(row == rows - 1, 0.0, pltpu.roll(a, rows - 1, 0)))
        tile[3] = 0.5 * (a + jnp.where(row == 0, 0.0, pltpu.roll(a, 1, 0)))
        tile[4] = 0.5 * (a + jnp.where(lane == depth - 1, 0.0, pltpu.roll(a, depth - 1, 1)))
        tile[5] = 0.5 * (a + jnp.where(lane == 0, 0.0, pltpu.roll(a, 1, 1)))
        for r in range(share):
            for n in range(6):
                faces[p, r, k, n] = jnp.broadcast_to(tile[n, pl.ds(me * share + r, 1), :], (SUB, depth))

    def face_loop(k, carry):
        for p in range(planes):
            face_step(k, p)
        return carry

    lax.fori_loop(0, terms, face_loop, 0)
    for p in range(planes):
        for r in range(share):
            total = faces[p, r, 0, 0]
            for n in range(1, 6):
                total = total + faces[p, r, 0, n]
            inverse[p, r] = 1.0 / total

    for q in range(planes):
        p = plane_at(planes - 1 - q)
        for d in range(1, groups):
            owner = group(-d)
            guess_copy(d, p, owner, me).wait_recv()

            @pl.when((p == planes - 1) & has_next)
            def _():
                rim_copy(True, d, owner).start()

            @pl.when((p == 0) & has_prev)
            def _():
                rim_copy(False, d, owner).start()


    lane = lax.broadcasted_iota(jnp.int32, (ROWS, depth), 1)

    def mix(step, p, base):
        image = jnp.zeros((width, band * depth), f32)
        second = jnp.zeros((width, band * depth), f32)
        for b in range(width // ROWS):
            begin = b * ROWS
            tops, rests = [], []
            for line in range(band):
                r = base + line

                def cells(x, y):
                    return field[step, x, y, begin:begin + ROWS, :]

                centre = cells(p + 1, r + 1)
                others = [
                    cells(p + 2, r + 1), cells(p, r + 1), cells(p + 1, r + 2), cells(p + 1, r),
                    jnp.where(lane == depth - 1, 0.0, pltpu.roll(centre, depth - 1, 1)),
                    jnp.where(lane == 0, 0.0, pltpu.roll(centre, 1, 1)),
                ]
                drops = [(centre - other).reshape(ROWS // SUB, SUB, depth) for other in others]
                highs, lows = [], []
                for k in range(terms):
                    acc = faces[p, r, k, 0][None] * drops[0]
                    for n in range(1, 6):
                        acc = acc + faces[p, r, k, n][None] * drops[n]
                    acc = acc.reshape(ROWS, depth)
                    if k == 0:
                        plain[line, begin:begin + ROWS, :] = acc
                    else:
                        top = acc.astype(bf16)
                        highs.append(top)
                        lows.append((acc - top.astype(f32)).astype(bf16))
                tops.append(jnp.concatenate(highs, axis=0))
                rests.append(jnp.concatenate(lows, axis=0))
            coarse = jnp.concatenate(tops, axis=1)
            fine = jnp.concatenate(rests, axis=1)
            both = jnp.dot(table[b], coarse, preferred_element_type=f32)
            image = image + both[:width] + jnp.dot(table[b, :width], fine, preferred_element_type=f32)
            second = second + both[width:]
        return image + second

    def x_copy(step, up, part):
        at, to, space = (planes, 0, here + 1) if up else (1, planes + 1, here - 1)
        span = pl.ds(1 + part * band, band)
        return remote(field.at[step, at, span], field.at[step, to, span],
                      x_sem, (step, 0 if up else 1, part), space, me)

    def y_copy(step, p, right):
        at, to, mode = (share, 0, me + 1) if right else (1, share + 1, me - 1)
        return remote(field.at[step, p + 1, at], field.at[step, p + 1, to],
                      y_sem, (step, 0 if right else 1, p), here, mode)

    def sol_copy(d, p, slot, target):
        return remote(field.at[ITERS - 1, p + 1, pl.ds(1, share), block(target)], back_s.at[slot, p],
                      sol_sem, (d, p), here, target)

    def upd_copy(d, p, part, slot, target):
        span = pl.ds(part * band, band)
        return remote(last.at[p, span, block(target)], back_u.at[slot, p, span],
                      upd_sem, (d, p, part), here, target)

    def await_rims(step, p, part):
        first = part == 0

        @pl.when((p == 0) & has_prev)
        def _():
            if step == 0:
                @pl.when(first)
                def _():
                    for d in range(groups):
                        rim_copy(True, d, group(-d)).wait_recv()
            else:
                x_copy(step, True, part).wait_recv()

        @pl.when((p == planes - 1) & has_next)
        def _():
            if step == 0:
                @pl.when(first)
                def _():
                    for d in range(groups):
                        rim_copy(False, d, group(-d)).wait_recv()
            else:
                x_copy(step, False, part).wait_recv()

        if step > 0:
            @pl.when(has_left & first)
            def _():
                y_copy(step, p, True).wait_recv()

            @pl.when(has_right & (part == bands - 1))
            def _():
                y_copy(step, p, False).wait_recv()

    for step in range(ITERS):
        def sweep(unit, carry, step=step):
            q, part = unit // bands, lax.rem(unit, bands)
            p = plane_at(q)
            base = part * band
            await_rims(step, p, part)
            if step == ITERS - 1:
                @pl.when(unit == planes * bands - 1)
                def _():
                    for d in range(1, groups):
                        sol_copy(d, p, me, group(d)).start()
            image = mix(step, p, base)
            if step == 0:
                @pl.when(unit == 0)
                def _():
                    for d in range(1, groups):
                        rhs_copy(d, group(-d), me).wait_recv()
            for line in range(band):
                r = base + line
                rest = rhs[p, r] - plain[line] - image[:, line * depth:(line + 1) * depth]
                rest = rest.reshape(width // SUB, SUB, depth) * (0.5 * inverse[p, r])[None]
                rest = rest.reshape(width, depth)
                if step < ITERS - 1:
                    field[step + 1, p + 1, r + 1] = field[step, p + 1, r + 1] + rest
                else:
                    last[p, r] = rest
            if step < ITERS - 1:
                @pl.when((p == planes - 1) & has_next)
                def _():
                    x_copy(step + 1, True, part).start()

                @pl.when((p == 0) & has_prev)
                def _():
                    x_copy(step + 1, False, part).start()

                @pl.when(has_right & (part == bands - 1))
                def _():
                    y_copy(step + 1, p, True).start()

                @pl.when(has_left & (part == 0))
                def _():
                    y_copy(step + 1, p, False).start()

            if step == ITERS - 2:
                @pl.when((part == bands - 1) & (q < planes - 1))
                def _():
                    for d in range(1, groups):
                        sol_copy(d, p, me, group(d)).start()
            if step == ITERS - 1:
                for d in range(1, groups):
                    upd_copy(d, p, part, me, group(d)).start()
            return carry

        lax.fori_loop(0, planes * bands, sweep, 0)

    def write(out, p, g, lines, base, cells):
        for r in range(lines):
            at = pl.ds(p * rows + g * share + base + r, blocks, stride=planes * rows)
            out[at, :] = cells[r][:blocks]

    for p in range(planes):
        write(half_out, p, me, share, 0, last[p, :, block(me)])
        write(sol_out, p, me, share, 0, field[ITERS - 1, p + 1, 1:share + 1, block(me)])
    for q in range(planes):
        p = plane_at(q)
        for d in range(1, groups):
            g = group(-d)
            sol_copy(d, p, g, me).wait_recv()
            write(sol_out, p, g, share, 0, back_s[g, p])
    for q in range(planes):
        p = plane_at(q)
        for d in range(1, groups):
            g = group(-d)
            for part in range(bands):
                upd_copy(d, p, part, g, me).wait_recv()
                write(half_out, p, g, band, part * band, back_u[g, p, pl.ds(part * band, band)])

    for d in range(1, groups):
        for p in range(planes):
            guess_copy(d, p, me, group(d)).wait_send()
            sol_copy(d, p, me, group(d)).wait_send()
            for part in range(bands):
                upd_copy(d, p, part, me, group(d)).wait_send()
        rhs_copy(d, me, group(d)).wait_send()
    for up, has in ((True, has_next), (False, has_prev)):
        @pl.when(has)
        def _():
            coef_copy(up).wait_send()
            for d in range(groups):
                rim_copy(up, d, group(-d)).wait_send()
            for step in range(1, ITERS):
                for part in range(bands):
                    x_copy(step, up, part).wait_send()
    for right, has in ((True, has_right), (False, has_left)):
        @pl.when(has)
        def _():
            for step in range(1, ITERS):
                for p in range(planes):
                    y_copy(step, p, right).wait_send()


def per_device(guess, source, mean_coef, fluct_coef, triples, coupling):
    blocks, planes, rows, depth = guess.shape
    groups, slabs = lax.axis_size("mode"), lax.axis_size("space")
    terms = fluct_coef.shape[0] + 1
    entries = triples.shape[1]
    share = rows // groups
    band = 2 if share % 2 == 0 else 1
    room = -(-blocks // 16) * 16
    while (room * groups) % 128:
        room += 16
    width = room * groups
    length = -(-entries // 128) * 128
    f32, bf16 = jnp.float32, jnp.bfloat16
    dims = (slabs, groups, blocks, room, planes, rows, depth, terms, entries)
    flat = jax.ShapeDtypeStruct((blocks * planes * rows, depth), f32)
    dma = pltpu.SemaphoreType.DMA
    vmem = pl.BlockSpec(memory_space=pltpu.VMEM)
    base, half = pl.pallas_call(
        functools.partial(kernel, dims),
        out_shape=(flat, flat),
        in_specs=[pl.BlockSpec(memory_space=pltpu.HBM)] * 6,
        out_specs=(vmem, vmem),
        scratch_shapes=[
            pltpu.VMEM(flat.shape, f32),
            pltpu.VMEM(flat.shape, f32),
            pltpu.VMEM(triples.shape, jnp.int32),
            pltpu.VMEM(coupling.shape, f32),
            dma((6,)),
            pltpu.VMEM((ITERS, planes + 2, share + 2, width, depth), f32),
            pltpu.VMEM((planes, share, width, depth), f32),
            pltpu.VMEM((groups, planes, share + 2, room, depth), f32),
            pltpu.VMEM((groups, planes, share, room, depth), f32),
            pltpu.VMEM((groups, planes, share, room, depth), f32),
            pltpu.VMEM((groups, planes, share, room, depth), f32),
            pltpu.VMEM((planes, share, width, depth), f32),
            pltpu.VMEM((terms, planes + 2, rows, depth), f32),
            pltpu.VMEM((6, rows, depth), f32),
            pltpu.VMEM((planes, share, terms, 6, SUB, depth), f32),
            pltpu.VMEM((planes, share, SUB, depth), f32),
            pltpu.VMEM((SUB, length), jnp.int32),
            pltpu.VMEM((width // ROWS, 2 * width, (terms - 1) * ROWS), bf16),
            pltpu.VMEM((band, width, depth), f32),
            dma((2, 2)),
            dma((2, groups, planes)),
            dma((2, groups)),
            dma((2, 2, groups)),
            dma((2, ITERS, 2, share // band)),
            dma((2, ITERS, 2, planes)),
            dma((2, groups, planes)),
            dma((2, groups, planes, share // band)),
        ],
        compiler_params=pltpu.CompilerParams(
            collective_id=0, has_side_effects=True, vmem_limit_bytes=62 * 1024 * 1024
        ),
    )(
        guess.reshape(flat.shape),
        source.reshape(flat.shape),
        mean_coef,
        fluct_coef,
        triples,
        coupling,
    )
    half = half.reshape(guess.shape)
    return base.reshape(guess.shape) + half, 2.0 * half


def solution(mesh):
    in_specs = (
        P("mode", "space", None, None),
        P("mode", "space", None, None),
        P("space", None, None),
        P(None, "space", None, None),
        P(),
        P(),
    )
    out_specs = (P("mode", "space", None, None), P("mode", "space", None, None))
    return jax.shard_map(
        per_device, mesh=mesh, in_specs=in_specs, out_specs=out_specs, check_vma=False
    )
```

```python
import functools

import jax
import jax.numpy as jnp
from jax import lax
from jax.experimental import pallas as pl
from jax.experimental.pallas import tpu as pltpu
from jax.sharding import PartitionSpec as P

ITERS = 3
MESH = pl.DeviceIdType.MESH
SUB = 8
ROWS = 32


def kernel(dims, guess_in, source_in, mean_in, fluct_in, triples_in, coupling_in, sol_out, half_out,
           guess, source, triples, coupling, in_sem,
           field, rhs, pack_g, pack_s, back_s, back_u, last, coef, tile, faces, inverse,
           pattern, table, plain,
           coef_sem, guess_sem, rhs_sem, rim_sem, x_sem, y_sem, sol_sem, upd_sem):
    slabs, groups, blocks, room, planes, rows, depth, terms, entries = dims
    share = rows // groups
    band = 2 if share % 2 == 0 else 1
    bands = share // band
    width = room * groups
    f32, bf16 = jnp.float32, jnp.bfloat16
    here = lax.axis_index("space")
    me = lax.axis_index("mode")
    has_prev, has_next = here > 0, here < slabs - 1
    has_left, has_right = me > 0, me < groups - 1
    even = lax.rem(here, 2) == 0

    def remote(src, dst, sems, index, space, mode):
        return pltpu.make_async_remote_copy(
            src_ref=src, dst_ref=dst, send_sem=sems.at[(0,) + index], recv_sem=sems.at[(1,) + index],
            device_id={"space": space, "mode": mode}, device_id_type=MESH)

    def group(offset):
        return lax.rem(me + offset + groups, groups)

    def block(owner):
        return pl.ds(pl.multiple_of(owner * room, SUB), room)

    def plane_at(q):
        return jnp.where(even, planes - 1 - q, q)

    inputs = [
        pltpu.make_async_copy(guess_in, guess, in_sem.at[0]),
        pltpu.make_async_copy(mean_in, coef.at[0, pl.ds(1, planes)], in_sem.at[1]),
        pltpu.make_async_copy(fluct_in, coef.at[pl.ds(1, terms - 1), pl.ds(1, planes)], in_sem.at[2]),
        pltpu.make_async_copy(source_in, source, in_sem.at[3]),
        pltpu.make_async_copy(triples_in, triples, in_sem.at[4]),
        pltpu.make_async_copy(coupling_in, coupling, in_sem.at[5]),
    ]
    for copy in inputs:
        copy.start()

    @pl.when(here == 0)
    def _():
        field[:, 0] = jnp.zeros((ITERS, share + 2, width, depth), f32)
        coef[:, 0] = jnp.zeros((terms, rows, depth), f32)

    @pl.when(here == slabs - 1)
    def _():
        field[:, planes + 1] = jnp.zeros((ITERS, share + 2, width, depth), f32)
        coef[:, planes + 1] = jnp.zeros((terms, rows, depth), f32)

    @pl.when(me == 0)
    def _():
        field[:, 1:planes + 1, 0] = jnp.zeros((ITERS, planes, width, depth), f32)

    @pl.when(me == groups - 1)
    def _():
        field[:, 1:planes + 1, share + 1] = jnp.zeros((ITERS, planes, width, depth), f32)

    barrier = pltpu.get_barrier_semaphore()

    @pl.when(has_prev)
    def _():
        pl.semaphore_signal(barrier, inc=1, device_id={"space": here - 1, "mode": me}, device_id_type=MESH)

    @pl.when(has_next)
    def _():
        pl.semaphore_signal(barrier, inc=1, device_id={"space": here + 1, "mode": me}, device_id_type=MESH)

    for d in range(1, groups):
        pl.semaphore_signal(barrier, inc=1, device_id={"space": here, "mode": group(d)}, device_id_type=MESH)

    tall = share + 1 if groups == 2 else share + 2

    def first_row(owner):
        return jnp.where(owner > 0, 0, 1) if groups == 2 else 0

    gap = jnp.zeros((room - blocks, depth), f32)

    def rows_of(ref, p, y):
        part = ref[pl.ds(p * rows + y, blocks, stride=planes * rows), :]
        return jnp.concatenate([part, gap], axis=0) if room > blocks else part

    def coef_copy(up):
        at, to, space = (planes, 0, here + 1) if up else (1, planes + 1, here - 1)
        return remote(coef.at[:, at], coef.at[:, to], coef_sem, (0 if up else 1,), space, me)

    def guess_copy(d, p, owner, target):
        start = first_row(target)
        return remote(
            pack_g.at[target, p, pl.ds(start, tall)],
            field.at[0, p + 1, pl.ds(start, tall), block(owner)],
            guess_sem, (d, p), here, target)

    def guess_row(p, target, at):
        y = target * share + at - 1
        inside = jnp.clip(y, 0, rows - 1)
        part = rows_of(guess, p, inside)
        return part if groups == 2 else jnp.where(y == inside, part, 0.0)

    inputs[0].wait()
    for q in range(planes):
        p = plane_at(planes - 1 - q)
        for d in range(1, groups):
            target = group(d)
            for r in range(tall):
                at = first_row(target) + r
                pack_g[target, p, at] = guess_row(p, target, at)
            if q == 0 and d == 1:
                pl.semaphore_wait(
                    barrier, groups - 1 + has_prev.astype(jnp.int32) + has_next.astype(jnp.int32))
            guess_copy(d, p, me, target).start()

    inputs[1].wait()
    inputs[2].wait()

    @pl.when(has_next)
    def _():
        coef_copy(True).start()

    @pl.when(has_prev)
    def _():
        coef_copy(False).start()

    def rim_copy(up, d, owner):
        at, to, space = (planes, 0, here + 1) if up else (1, planes + 1, here - 1)
        span = pl.ds(1, share)
        return remote(field.at[0, at, span, block(owner)], field.at[0, to, span, block(owner)],
                      rim_sem, (0 if up else 1, d), space, me)

    for p in range(planes):
        for r in range(tall):
            at = first_row(me) + r
            field[0, p + 1, at, block(me)] = guess_row(p, me, at)

    @pl.when(has_next)
    def _():
        rim_copy(True, 0, me).start()

    @pl.when(has_prev)
    def _():
        rim_copy(False, 0, me).start()

    inputs[3].wait()
    for d in range(groups):
        target = group(d)
        for p in range(planes):
            for r in range(share):
                part = rows_of(source, p, target * share + r)
                if d == 0:
                    rhs[p, r, block(me)] = part
                else:
                    pack_s[target, p, r] = part

    inputs[4].wait()
    inputs[5].wait()
    pattern[...] = jnp.full(pattern.shape, -1, jnp.int32)
    pattern[0:3, 0:entries] = triples[...]
    length = pattern.shape[1]

    def spread(i):
        shift = jnp.zeros_like(i)
        for g in range(1, groups):
            shift = shift + jnp.where(i >= g * blocks, room - blocks, 0)
        return i + shift

    owner_row = spread(pattern[0:1, :])
    partner = spread(pattern[1:2, :])
    chunk = (terms - 1) * ROWS
    column = partner + (partner // ROWS) * (chunk - ROWS) + (pattern[2:3, :] - 1) * ROWS
    value = jnp.concatenate([coupling[...].reshape(1, entries), jnp.zeros((1, length - entries), f32)], axis=1)
    high = value.astype(bf16).astype(f32)
    low = value - high
    hit = lax.broadcasted_iota(jnp.int32, (width, length), 0) == owner_row
    picks = jnp.concatenate(
        [jnp.where(hit, high, 0.0).astype(bf16), jnp.where(hit, low, 0.0).astype(bf16)], axis=0)
    order = lax.broadcasted_iota(jnp.int32, (chunk, length), 0)
    for b in range(width // ROWS):
        chosen = jnp.where(order == column - b * chunk, 1.0, 0.0).astype(bf16)
        both = lax.dot_general(picks, chosen, (((1,), (1,)), ((), ())), preferred_element_type=f32)
        entry = both[:width] + both[width:]
        top = entry.astype(bf16)
        table[b, :width, :] = top
        table[b, width:, :] = (entry - top.astype(f32)).astype(bf16)

    def rhs_copy(d, p, owner, target):
        return remote(pack_s.at[target, p], rhs.at[p, :, block(owner)], rhs_sem, (d, p), here, target)

    for q in range(planes):
        for d in range(1, groups):
            rhs_copy(d, plane_at(q), me, group(d)).start()

    @pl.when(has_prev)
    def _():
        coef_copy(True).wait_recv()

    @pl.when(has_next)
    def _():
        coef_copy(False).wait_recv()

    def face_step(k, p):
        a = coef[k, p + 1]
        row = lax.broadcasted_iota(jnp.int32, a.shape, 0)
        lane = lax.broadcasted_iota(jnp.int32, a.shape, 1)
        tile[0] = 0.5 * (a + coef[k, p + 2])
        tile[1] = 0.5 * (a + coef[k, p])
        tile[2] = 0.5 * (a + jnp.where(row == rows - 1, 0.0, pltpu.roll(a, rows - 1, 0)))
        tile[3] = 0.5 * (a + jnp.where(row == 0, 0.0, pltpu.roll(a, 1, 0)))
        tile[4] = 0.5 * (a + jnp.where(lane == depth - 1, 0.0, pltpu.roll(a, depth - 1, 1)))
        tile[5] = 0.5 * (a + jnp.where(lane == 0, 0.0, pltpu.roll(a, 1, 1)))
        for r in range(share):
            for n in range(6):
                faces[p, r, k, n] = jnp.broadcast_to(tile[n, pl.ds(me * share + r, 1), :], (SUB, depth))

    def face_loop(k, carry):
        for p in range(planes):
            face_step(k, p)
        return carry

    lax.fori_loop(0, terms, face_loop, 0)
    for p in range(planes):
        for r in range(share):
            total = faces[p, r, 0, 0]
            for n in range(1, 6):
                total = total + faces[p, r, 0, n]
            inverse[p, r] = 1.0 / total

    for q in range(planes):
        p = plane_at(planes - 1 - q)
        for d in range(1, groups):
            owner = group(-d)
            guess_copy(d, p, owner, me).wait_recv()

            @pl.when((p == planes - 1) & has_next)
            def _():
                rim_copy(True, d, owner).start()

            @pl.when((p == 0) & has_prev)
            def _():
                rim_copy(False, d, owner).start()


    lane = lax.broadcasted_iota(jnp.int32, (ROWS, depth), 1)

    def mix(step, p, base):
        image = jnp.zeros((width, band * depth), f32)
        second = jnp.zeros((width, band * depth), f32)
        for b in range(width // ROWS):
            begin = b * ROWS
            tops, rests = [], []
            for line in range(band):
                r = base + line

                def cells(x, y):
                    return field[step, x, y, begin:begin + ROWS, :]

                centre = cells(p + 1, r + 1)
                others = [
                    cells(p + 2, r + 1), cells(p, r + 1), cells(p + 1, r + 2), cells(p + 1, r),
                    jnp.where(lane == depth - 1, 0.0, pltpu.roll(centre, depth - 1, 1)),
                    jnp.where(lane == 0, 0.0, pltpu.roll(centre, 1, 1)),
                ]
                drops = [(centre - other).reshape(ROWS // SUB, SUB, depth) for other in others]
                highs, lows = [], []
                for k in range(terms):
                    acc = faces[p, r, k, 0][None] * drops[0]
                    for n in range(1, 6):
                        acc = acc + faces[p, r, k, n][None] * drops[n]
                    acc = acc.reshape(ROWS, depth)
                    if k == 0:
                        plain[line, begin:begin + ROWS, :] = acc
                    else:
                        top = acc.astype(bf16)
                        highs.append(top)
                        lows.append((acc - top.astype(f32)).astype(bf16))
                tops.append(jnp.concatenate(highs, axis=0))
                rests.append(jnp.concatenate(lows, axis=0))
            coarse = jnp.concatenate(tops, axis=1)
            fine = jnp.concatenate(rests, axis=1)
            both = jnp.dot(table[b], coarse, preferred_element_type=f32)
            image = image + both[:width] + jnp.dot(table[b, :width], fine, preferred_element_type=f32)
            second = second + both[width:]
        return image + second

    def x_copy(step, up, part):
        at, to, space = (planes, 0, here + 1) if up else (1, planes + 1, here - 1)
        span = pl.ds(1 + part * band, band)
        return remote(field.at[step, at, span], field.at[step, to, span],
                      x_sem, (step, 0 if up else 1, part), space, me)

    def y_copy(step, p, right):
        at, to, mode = (share, 0, me + 1) if right else (1, share + 1, me - 1)
        return remote(field.at[step, p + 1, at], field.at[step, p + 1, to],
                      y_sem, (step, 0 if right else 1, p), here, mode)

    def sol_copy(d, p, slot, target):
        return remote(field.at[ITERS - 1, p + 1, pl.ds(1, share), block(target)], back_s.at[slot, p],
                      sol_sem, (d, p), here, target)

    def upd_copy(d, p, part, slot, target):
        span = pl.ds(part * band, band)
        return remote(last.at[p, span, block(target)], back_u.at[slot, p, span],
                      upd_sem, (d, p, part), here, target)

    def await_rims(step, p, part):
        first = part == 0

        @pl.when((p == 0) & has_prev)
        def _():
            if step == 0:
                @pl.when(first)
                def _():
                    for d in range(groups):
                        rim_copy(True, d, group(-d)).wait_recv()
            else:
                x_copy(step, True, part).wait_recv()

        @pl.when((p == planes - 1) & has_next)
        def _():
            if step == 0:
                @pl.when(first)
                def _():
                    for d in range(groups):
                        rim_copy(False, d, group(-d)).wait_recv()
            else:
                x_copy(step, False, part).wait_recv()

        if step > 0:
            @pl.when(has_left & first)
            def _():
                y_copy(step, p, True).wait_recv()

            @pl.when(has_right & (part == bands - 1))
            def _():
                y_copy(step, p, False).wait_recv()

    for step in range(ITERS):
        def sweep(unit, carry, step=step):
            q, part = unit // bands, lax.rem(unit, bands)
            p = plane_at(q)
            base = part * band
            await_rims(step, p, part)
            if step == ITERS - 1:
                @pl.when(unit == planes * bands - 1)
                def _():
                    for d in range(1, groups):
                        sol_copy(d, p, me, group(d)).start()
            image = mix(step, p, base)
            if step == 0:
                @pl.when(part == 0)
                def _():
                    for d in range(1, groups):
                        rhs_copy(d, p, group(-d), me).wait_recv()
            for line in range(band):
                r = base + line
                rest = rhs[p, r] - plain[line] - image[:, line * depth:(line + 1) * depth]
                rest = rest.reshape(width // SUB, SUB, depth) * (0.5 * inverse[p, r])[None]
                rest = rest.reshape(width, depth)
                if step < ITERS - 1:
                    field[step + 1, p + 1, r + 1] = field[step, p + 1, r + 1] + rest
                else:
                    last[p, r] = rest
            if step < ITERS - 1:
                @pl.when((p == planes - 1) & has_next)
                def _():
                    x_copy(step + 1, True, part).start()

                @pl.when((p == 0) & has_prev)
                def _():
                    x_copy(step + 1, False, part).start()

                @pl.when(has_right & (part == bands - 1))
                def _():
                    y_copy(step + 1, p, True).start()

                @pl.when(has_left & (part == 0))
                def _():
                    y_copy(step + 1, p, False).start()

            if step == ITERS - 2:
                @pl.when((part == bands - 1) & (q < planes - 1))
                def _():
                    for d in range(1, groups):
                        sol_copy(d, p, me, group(d)).start()
            if step == ITERS - 1:
                for d in range(1, groups):
                    upd_copy(d, p, part, me, group(d)).start()
            return carry

        lax.fori_loop(0, planes * bands, sweep, 0)

    def write(out, p, g, lines, base, cells):
        for r in range(lines):
            at = pl.ds(p * rows + g * share + base + r, blocks, stride=planes * rows)
            out[at, :] = cells[r][:blocks]

    for p in range(planes):
        write(half_out, p, me, share, 0, last[p, :, block(me)])
        write(sol_out, p, me, share, 0, field[ITERS - 1, p + 1, 1:share + 1, block(me)])
    for q in range(planes):
        p = plane_at(q)
        for d in range(1, groups):
            g = group(-d)
            sol_copy(d, p, g, me).wait_recv()
            write(sol_out, p, g, share, 0, back_s[g, p])
    for q in range(planes):
        p = plane_at(q)
        for d in range(1, groups):
            g = group(-d)
            for part in range(bands):
                upd_copy(d, p, part, g, me).wait_recv()
                write(half_out, p, g, band, part * band, back_u[g, p, pl.ds(part * band, band)])

    for d in range(1, groups):
        for p in range(planes):
            guess_copy(d, p, me, group(d)).wait_send()
            sol_copy(d, p, me, group(d)).wait_send()
            for part in range(bands):
                upd_copy(d, p, part, me, group(d)).wait_send()
            rhs_copy(d, p, me, group(d)).wait_send()
    for up, has in ((True, has_next), (False, has_prev)):
        @pl.when(has)
        def _():
            coef_copy(up).wait_send()
            for d in range(groups):
                rim_copy(up, d, group(-d)).wait_send()
            for step in range(1, ITERS):
                for part in range(bands):
                    x_copy(step, up, part).wait_send()
    for right, has in ((True, has_right), (False, has_left)):
        @pl.when(has)
        def _():
            for step in range(1, ITERS):
                for p in range(planes):
                    y_copy(step, p, right).wait_send()


def per_device(guess, source, mean_coef, fluct_coef, triples, coupling):
    blocks, planes, rows, depth = guess.shape
    groups, slabs = lax.axis_size("mode"), lax.axis_size("space")
    terms = fluct_coef.shape[0] + 1
    entries = triples.shape[1]
    share = rows // groups
    band = 2 if share % 2 == 0 else 1
    room = -(-blocks // 16) * 16
    while (room * groups) % 128:
        room += 16
    width = room * groups
    length = -(-entries // 128) * 128
    f32, bf16 = jnp.float32, jnp.bfloat16
    dims = (slabs, groups, blocks, room, planes, rows, depth, terms, entries)
    flat = jax.ShapeDtypeStruct((blocks * planes * rows, depth), f32)
    dma = pltpu.SemaphoreType.DMA
    vmem = pl.BlockSpec(memory_space=pltpu.VMEM)
    base, half = pl.pallas_call(
        functools.partial(kernel, dims),
        out_shape=(flat, flat),
        in_specs=[pl.BlockSpec(memory_space=pltpu.HBM)] * 6,
        out_specs=(vmem, vmem),
        scratch_shapes=[
            pltpu.VMEM(flat.shape, f32),
            pltpu.VMEM(flat.shape, f32),
            pltpu.VMEM(triples.shape, jnp.int32),
            pltpu.VMEM(coupling.shape, f32),
            dma((6,)),
            pltpu.VMEM((ITERS, planes + 2, share + 2, width, depth), f32),
            pltpu.VMEM((planes, share, width, depth), f32),
            pltpu.VMEM((groups, planes, share + 2, room, depth), f32),
            pltpu.VMEM((groups, planes, share, room, depth), f32),
            pltpu.VMEM((groups, planes, share, room, depth), f32),
            pltpu.VMEM((groups, planes, share, room, depth), f32),
            pltpu.VMEM((planes, share, width, depth), f32),
            pltpu.VMEM((terms, planes + 2, rows, depth), f32),
            pltpu.VMEM((6, rows, depth), f32),
            pltpu.VMEM((planes, share, terms, 6, SUB, depth), f32),
            pltpu.VMEM((planes, share, SUB, depth), f32),
            pltpu.VMEM((SUB, length), jnp.int32),
            pltpu.VMEM((width // ROWS, 2 * width, (terms - 1) * ROWS), bf16),
            pltpu.VMEM((band, width, depth), f32),
            dma((2, 2)),
            dma((2, groups, planes)),
            dma((2, groups, planes)),
            dma((2, 2, groups)),
            dma((2, ITERS, 2, share // band)),
            dma((2, ITERS, 2, planes)),
            dma((2, groups, planes)),
            dma((2, groups, planes, share // band)),
        ],
        compiler_params=pltpu.CompilerParams(
            collective_id=0, has_side_effects=True, vmem_limit_bytes=62 * 1024 * 1024
        ),
    )(
        guess.reshape(flat.shape),
        source.reshape(flat.shape),
        mean_coef,
        fluct_coef,
        triples,
        coupling,
    )
    half = half.reshape(guess.shape)
    return base.reshape(guess.shape) + half, 2.0 * half


def solution(mesh):
    in_specs = (
        P("mode", "space", None, None),
        P("mode", "space", None, None),
        P("space", None, None),
        P(None, "space", None, None),
        P(),
        P(),
    )
    out_specs = (P("mode", "space", None, None), P("mode", "space", None, None))
    return jax.shard_map(
        per_device, mesh=mesh, in_specs=in_specs, out_specs=out_specs, check_vma=False
    )
```
